128 devices in a mesh: dp: 8 (over z_hi, y), tp: 16 (over z_lo, x, core).
Axes of the slice: x: 4, y: 4, z: 4 (z_hi: 2, z_lo: 2; z = z_hi * 2 + z_lo), core: 2. Of those that a mesh axis runs over, the one named last changes fastest.
Arguments:
- request_latent_cache: bfloat16 [2048, 192, 576], P(('dp', 'tp')), may hold values from -6 to 6
- lengths: int32 [2048], P(('dp', 'tp')), may hold values from 64 to 192, as said below
- queries: bfloat16 [2048, 2, 128, 576], P(('dp', 'tp')), may hold values from -6 to 6
- incoming_keys: bfloat16 [2048, 2, 576], P(('dp', 'tp')), may hold values from -6 to 6
- hidden_in: bfloat16 [2048, 2, 3584], P(('dp', 'tp')), may hold values from -4 to 4
- value_up_weight: bfloat16 [128, 512, 128], P('tp'), may hold values from -0.25 to 0.25
- w_out: bfloat16 [16384, 3584], P('tp'), may hold values from -0.375 to 0.375
- norm_gain: float32 [3584], replicated, may hold values from 0.25 to 1.75
- w_gate: bfloat16 [3584, 10240], P(None, 'tp'), may hold values from -0.09375 to 0.09375
- w_up: bfloat16 [3584, 10240], P(None, 'tp'), may hold values from -0.09375 to 0.09375
- w_down: bfloat16 [10240, 3584], P('tp'), may hold values from -0.15625 to 0.15625
- partner: int32 [8, 16], P(None, 'tp'), may hold values from 0 to 7, as said below
- moved_request: int32 [128], P(('dp', 'tp')), may hold values from 0 to 15
- moved_pages: int32 [128], P(('dp', 'tp')), may hold values from 1 to 2, as said below
Outputs:
- layer_out: bfloat16 [2048, 2, 3584], P(('dp', 'tp'))
- moved_cache: bfloat16 [256, 64, 576], P(('dp', 'tp'))
The draws below stay inside these ranges and needn't reach their ends.
Inputs may be any that keep to these rules, and one draw needn't show every extreme that they name: `lengths`: some request holds 192 rows in every draw. For each tp index t, partner[d, t] = d XOR c[t] for one c[t] of 1 to 7, so partner[partner[d, t], t] = d. `moved_pages`: device 0 hands over 2 pages in every draw.
All inputs are finite; a program needn't handle non-finite values.
Results may differ from the reference program's by a relative error of at most 0.025.
Values may be sent and summed in bfloat16 or wider, within the bound.
No kernel may reach another device: no remote copies, remote signals or barrier semaphores. Data moves between devices by JAX's collectives and lax.ppermute only.
A program may use at most 128 MiB of HBM per device.

```python
import jax
import jax.numpy as jnp
from jax import lax

D = 3584
FF = 10240
HEAD_COUNT = 128
LATENT_WIDTH = 512
VALUE_WIDTH = 128
REQ_DEV = 16
LMAX = 192
STEPS = 2
PAGE = 64
MIG_MAX = 2
LAT = 576
REQUESTS = 2048
N_DP = 8
N_TP = 16


score_root = 192.0 ** 0.5


def shared_rows(key):
    sign_key, first_key, offset_key = jax.random.split(key, 3)
    signs = (2 * jax.random.randint(sign_key, (REQUESTS, LAT), 0, 2) - 1).astype(jnp.float32)
    first = jax.random.randint(first_key, (REQUESTS,), 0, PAGE)
    second = (first + jax.random.randint(offset_key, (REQUESTS,), 1, PAGE)) % PAGE
    return (signs, first, second)


def column_weights():
    column_list = jnp.arange(LAT, dtype=jnp.int32)
    weight_table = jnp.where(column_list < LATENT_WIDTH, 2.0, 6.0).astype(jnp.float32)
    flips = (1 - 2 * (column_list % 2)).astype(jnp.float32)
    return (weight_table, flips)


def draw_request_latent_cache(key, part):
    signs, first, second = shared_rows(key)
    key = jax.random.fold_in(key, 21)
    shape = (REQUESTS, LMAX, LAT)
    base = jax.random.truncated_normal(key, -6.0, 6.0, shape, jnp.float32)
    weight_table, flips = column_weights()
    positions = jnp.arange(LMAX, dtype=jnp.int32)[None, :, None]
    row_one = (signs * weight_table)[:, None, :]
    row_two = row_one * flips
    cache = jnp.where(positions == first[:, None, None], row_one, base)
    cache = jnp.where(positions == second[:, None, None], row_two, cache)
    return cache.astype(jnp.bfloat16)


def draw_queries(key, part):
    signs, first, second = shared_rows(key)
    key = jax.random.fold_in(key, 22)
    base_key = jax.random.fold_in(key, 0)
    pick_key = jax.random.fold_in(key, 2)
    head_key = jax.random.fold_in(key, 3)
    level_key = jax.random.fold_in(key, 4)
    spread_key = jax.random.fold_in(key, 5)
    shape = (REQUESTS, STEPS, HEAD_COUNT, LAT)
    base = jax.random.truncated_normal(base_key, -6.0, 6.0, shape, jnp.float32)
    picked = (jax.random.randint(pick_key, (REQUESTS,), 0, 4) == 0).at[0].set(True)
    heads = (jax.random.randint(head_key, (REQUESTS, STEPS, HEAD_COUNT), 0, 16) == 0).at[0, 0, 0].set(True)
    aligned = picked[:, None, None] & heads
    level = jax.random.randint(level_key, (REQUESTS, STEPS, HEAD_COUNT), 0, 4).at[0, 0, 0].set(3)
    tops = jnp.array([110.0, 160.0, 220.0, 290.0], jnp.float32)[level]
    spreads = jax.random.uniform(spread_key, (REQUESTS, STEPS, HEAD_COUNT), jnp.float32, 1.0, 3.0)
    weight_table, flips = column_weights()
    unit = score_root / jnp.sum(weight_table)
    first_part = jnp.minimum(tops * unit, 2.9)
    second_part = first_part - spreads * unit
    lined = signs[:, None, None, :] * (first_part[..., None] + second_part[..., None] * flips)
    result = jnp.where(aligned[..., None], lined, base)
    return result.astype(jnp.bfloat16)


def draw_lengths(key, part):
    key = jax.random.fold_in(key, 11)
    first, second = jax.random.split(key)
    devices = REQUESTS // REQ_DEV
    level = jax.random.randint(first, (devices, 1), 1, 5)
    base = jax.random.randint(second, (devices, REQ_DEV), 1, LMAX + 1)
    lens = jnp.maximum(base * level // 4, PAGE).reshape(REQUESTS)
    return lens.at[0].set(LMAX).astype(jnp.int32)


def draw_partner(key, part):
    key = jax.random.fold_in(key, 12)
    offsets = jax.random.randint(key, (N_TP,), 1, N_DP).astype(jnp.int32)
    offsets = offsets.at[0].set(N_DP // 2)
    return jnp.bitwise_xor(jnp.arange(N_DP, dtype=jnp.int32)[:, None], offsets[None, :]).astype(jnp.int32)


def draw_moved_pages(key, part):
    key = jax.random.fold_in(key, 13)
    counts = jax.random.randint(key, (REQUESTS // REQ_DEV,), 1, MIG_MAX + 1)
    return counts.at[0].set(MIG_MAX).astype(jnp.int32)


def touch_ends(entries, rng, smallest, high):
    shape = entries.shape
    spot = [jax.random.randint(jax.random.fold_in(rng, axis), (), 0, shape[axis]) for axis in range(len(shape))]
    entries = entries.at[tuple(spot)].set(smallest)
    longest = shape.index(max(shape))
    spot[longest] = (spot[longest] + 1) % shape[longest]
    return entries.at[tuple(spot)].set(high)


def level_of(stream_key, extent, cuts, smallest, high):
    loudness = 1.0
    for position, shards_of in cuts:
        heights = jax.random.uniform(jax.random.fold_in(jax.random.fold_in(stream_key, 6), position), (shards_of,), jnp.float32, smallest / len(cuts), high / len(cuts))
        loudness = loudness * jnp.repeat(jnp.exp(heights), extent[position] // shards_of).reshape((-1,) + (1,) * (len(extent) - 1 - position))
    return loudness


def scatter_about(key, dims, spread, bound, cuts=(), kind=jnp.bfloat16):
    entries = spread * jax.random.normal(key, dims, jnp.float32)
    if cuts:
        entries = entries * level_of(key, dims, cuts, -0.22, 0.18)
    return jnp.clip(entries, -bound, bound).astype(kind)


def setup_inputs(seed: int = 0) -> dict:
    seeds = jax.random.split(jax.random.key(seed), 15)
    request_latent_cache = draw_request_latent_cache(jax.random.fold_in(seeds[14], 71), 0)
    lengths = draw_lengths(jax.random.fold_in(seeds[14], 71), 0)
    queries = draw_queries(jax.random.fold_in(seeds[14], 71), 0)
    incoming_keys = scatter_about(seeds[3], (REQUESTS, STEPS, LAT), 1.0, 6.0, ((0, 128),))
    hidden_in = scatter_about(seeds[4], (REQUESTS, STEPS, D), 0.5, 4.0, ((0, 128),))
    value_up_weight = scatter_about(seeds[5], (HEAD_COUNT, LATENT_WIDTH, VALUE_WIDTH), LATENT_WIDTH ** -0.5, 0.25, ((0, 16),))
    w_out = scatter_about(seeds[6], (HEAD_COUNT * VALUE_WIDTH, D), (HEAD_COUNT * VALUE_WIDTH // 64) ** -0.5, 0.375, ((0, 16),))
    norm_gain = jnp.clip(1.0 + 0.15 * jax.random.normal(seeds[7], (D,), jnp.float32), 0.25, 1.75)
    w_gate = scatter_about(seeds[8], (D, FF), D ** -0.5, 0.09375, ((1, 16),))
    w_up = scatter_about(seeds[9], (D, FF), D ** -0.5, 0.09375, ((1, 16),))
    w_down = scatter_about(seeds[10], (FF, D), (FF // 8) ** -0.5, 0.15625, ((0, 16),))
    partner = draw_partner(jax.random.fold_in(seeds[14], 71), 0)
    moved_request = touch_ends(jax.random.randint(seeds[12], (N_DP * N_TP,), 0, REQ_DEV), jax.random.fold_in(seeds[12], 1), 0, REQ_DEV - 1).astype(jnp.int32)
    moved_pages = draw_moved_pages(jax.random.fold_in(seeds[14], 71), 0)
    return dict(request_latent_cache=request_latent_cache, lengths=lengths, queries=queries, incoming_keys=incoming_keys, hidden_in=hidden_in, value_up_weight=value_up_weight, w_out=w_out, norm_gain=norm_gain, w_gate=w_gate, w_up=w_up, w_down=w_down, partner=partner, moved_request=moved_request, moved_pages=moved_pages)


score_scale = 192.0 ** (-0.5)
masked_score = -1e+30
norm_eps = 1e-06

def attend_latent(group):
    block_cache, lens, query_rows, fresh_keys = group
    key_matrix = jnp.concatenate([block_cache, fresh_keys], axis=1).astype(jnp.float32)
    scores = jnp.einsum('bshc,btc->bsht', query_rows.astype(jnp.float32), key_matrix) * score_scale
    positions = jnp.arange(LMAX + STEPS, dtype=jnp.int32)
    step_ids = jnp.arange(STEPS, dtype=jnp.int32)
    visible = jnp.where(positions[None, None, :] < LMAX, positions[None, None, :] < lens[:, None, None], positions[None, None, :] - LMAX <= step_ids[None, :, None])
    scores = jnp.where(visible[:, :, None, :], scores, masked_score)
    peak = lax.optimization_barrier(jnp.max(scores, axis=-1, keepdims=True))
    weight_table = jnp.exp(scores - peak)
    probabilities = (weight_table / lax.optimization_barrier(jnp.sum(weight_table, axis=-1, keepdims=True))).astype(jnp.bfloat16)
    latent_rows = jnp.einsum('uaef,ufv->uaev', probabilities.astype(jnp.float32), key_matrix[..., :LATENT_WIDTH])
    return latent_rows.astype(jnp.bfloat16)

def group_total(left, right, groups):
    rows_all = left.shape[0]
    width_in = left.shape[1] // groups
    left_groups = left.reshape(rows_all, groups, width_in)
    right_groups = right.reshape(groups, width_in, right.shape[1])

    def accumulate(running, group_id):
        product = jnp.dot(lax.dynamic_index_in_dim(left_groups, group_id, 1, keepdims=False), lax.dynamic_index_in_dim(right_groups, group_id, 0, keepdims=False), preferred_element_type=jnp.float32)
        rounded = lax.optimization_barrier(product.astype(jnp.bfloat16))
        return (running + rounded.astype(jnp.float32), None)
    start_sum = jnp.zeros((rows_all, right.shape[1]), jnp.float32)
    running, unused = lax.scan(accumulate, start_sum, jnp.arange(groups, dtype=jnp.int32))
    return running

def reference(request_latent_cache, lengths, queries, incoming_keys, hidden_in, value_up_weight, w_out, norm_gain, w_gate, w_up, w_down, partner, moved_request, moved_pages):
    groups = REQUESTS // REQ_DEV
    latent_output = lax.map(attend_latent, (request_latent_cache.reshape(groups, REQ_DEV, LMAX, LAT), lengths.reshape(groups, REQ_DEV), queries.reshape(groups, REQ_DEV, STEPS, HEAD_COUNT, LAT), incoming_keys.reshape(groups, REQ_DEV, STEPS, LAT)))
    row_list = REQUESTS * STEPS
    latent_output = latent_output.reshape(row_list, HEAD_COUNT, LATENT_WIDTH)
    values = jnp.einsum('nhc,hcv->nhv', latent_output.astype(jnp.float32), value_up_weight.astype(jnp.float32)).astype(jnp.bfloat16)
    attn = group_total(values.reshape(row_list, HEAD_COUNT * VALUE_WIDTH), w_out, N_TP)
    residual = hidden_in.reshape(row_list, D).astype(jnp.float32) + attn
    normed = (residual * lax.rsqrt(lax.optimization_barrier(jnp.mean(residual * residual, axis=-1, keepdims=True)) + norm_eps) * norm_gain).astype(jnp.bfloat16)
    gate = jnp.dot(normed, w_gate, preferred_element_type=jnp.float32)
    up_part = jnp.dot(normed, w_up, preferred_element_type=jnp.float32)
    hidden = (jax.nn.silu(gate) * up_part).astype(jnp.bfloat16)
    layer_out = (residual + group_total(hidden, w_down, N_TP)).astype(jnp.bfloat16)
    device_ids = jnp.arange(N_DP * N_TP, dtype=jnp.int32)
    tp_ids = device_ids % N_TP
    source = partner[device_ids // N_TP, tp_ids] * N_TP + tp_ids
    request_ids = source * REQ_DEV + moved_request[source]
    blocks = request_latent_cache[request_ids, :MIG_MAX * PAGE].reshape(N_DP * N_TP, MIG_MAX, PAGE, LAT)
    keep = jnp.arange(MIG_MAX, dtype=jnp.int32)[None, :] < moved_pages[source][:, None]
    blocks = jnp.where(keep[:, :, None, None], blocks, jnp.zeros_like(blocks))
    return (layer_out.reshape(REQUESTS, STEPS, D), blocks.reshape(N_DP * N_TP * MIG_MAX, PAGE, LAT))
```

```python
import functools

import jax
import jax.numpy as jnp
from jax import lax
from jax.experimental import pallas as pl
from jax.experimental.pallas import tpu as pltpu
from jax.sharding import PartitionSpec as P

LATENT_WIDTH = 512
PAGE = 64
MIG_MAX = 2
N_X = 4
N_Z = 4
N_Y = 4
GRID = ("dp", "tp")
T_PAD = 208
GROUP = 4

score_scale = 192.0 ** (-0.5)
masked_score = -1e30
norm_eps = 1e-06


def place(index):
    d, t = index // 16, index % 16
    return (d // 4) * 2 + t // 8, d % 4, (t // 2) % 4, t % 2


def index_of(z, y, x, c):
    z, y, x = z % N_Z, y % N_Y, x % N_X
    return ((z // 2) * 4 + y) * 16 + (z % 2) * 8 + x * 2 + c


def shift(value, dx=0, dz=0):
    pairs = []
    for i in range(128):
        z, y, x, c = place(i)
        pairs.append((i, index_of(z + dz, y, x + dx, c)))
    return lax.ppermute(value, GRID, pairs)


def swap_cores(value):
    return lax.ppermute(value, "tp", [(t, t ^ 1) for t in range(16)])


def attend_kernel(where_ref, lens_ref, q_ref, cache_ref, fresh_ref, *rest, first_request):
    *outs, keys, rows = rest
    i = pl.program_id(0)
    reqs, steps, width, heads = q_ref.shape
    capacity = cache_ref.shape[1]
    total = keys.shape[1]

    @pl.when(i == 0)
    def _():
        keys[...] = jnp.zeros_like(keys)

    position = lax.broadcasted_iota(jnp.int32, (total, steps * heads), 0)
    column = lax.broadcasted_iota(jnp.int32, (total, steps * heads), 1)
    fresh_ok = (position >= capacity) & (position - capacity <= column // heads)
    z, x, c = where_ref[0], where_ref[1], where_ref[2]
    group = keys.shape[0]
    for first in range(0, reqs, group):
        scores, probs = [], []
        for g in range(group):
            r = first + g
            keys[g, 0:capacity, :] = cache_ref[r]
            keys[g, capacity : capacity + steps, :] = fresh_ref[r]
            q = jnp.concatenate([q_ref[r, s] for s in range(steps)], axis=1)
            scores.append(jnp.dot(keys[g], q, preferred_element_type=jnp.float32))
        for g in range(group):
            visible = (position < lens_ref[first_request + i * reqs + first + g]) | fresh_ok
            masked = jnp.where(visible, scores[g] * score_scale, masked_score)
            peak = jnp.max(masked, axis=0, keepdims=True)
            weight = jnp.exp(masked - peak)
            inverse = 1.0 / jnp.sum(weight, axis=0, keepdims=True)
            probs.append((weight * inverse).astype(jnp.bfloat16))
        for g in range(group):
            latent = lax.dot_general(
                probs[g],
                keys[g, :, :LATENT_WIDTH],
                (((0,), (0,)), ((), ())),
                preferred_element_type=jnp.float32,
            )
            rows[g] = latent
        for g in range(group):
            at = (i * reqs + first + g) * steps
            for side in range(2):
                zz = z if side == 0 else 1 - z
                for rel in range(N_X):
                    out = outs[side * N_X + rel]
                    chip = zz * 64 + lax.rem(x + rel, N_X) * 16
                    for s in range(steps):
                        picked = [
                            rows[g, pl.ds(pl.multiple_of(s * heads + chip + core * 8, 8), 8), :]
                            for core in (c, 1 - c)
                        ]
                        out[at + s] = jnp.concatenate(picked, axis=0).astype(jnp.bfloat16)


def attend(where, lengths, queries, cache, fresh, first, count):
    reqs, steps, width, heads = queries.shape
    capacity = cache.shape[1]
    part = 4
    n = count * steps
    base = first // part
    return pl.pallas_call(
        functools.partial(attend_kernel, first_request=first),
        grid_spec=pltpu.PrefetchScalarGridSpec(
            num_scalar_prefetch=2,
            grid=(count // part,),
            in_specs=[
                pl.BlockSpec((part, steps, width, heads), lambda i, w, l: (base + i, 0, 0, 0)),
                pl.BlockSpec((part, capacity, width), lambda i, w, l: (base + i, 0, 0)),
                pl.BlockSpec((part, steps, width), lambda i, w, l: (base + i, 0, 0)),
            ],
            out_specs=[pl.BlockSpec((n, 16, LATENT_WIDTH), lambda i, w, l: (0, 0, 0))] * (2 * N_X),
            scratch_shapes=[
                pltpu.VMEM((GROUP, T_PAD, width), jnp.bfloat16),
                pltpu.VMEM((GROUP, steps * heads, LATENT_WIDTH), jnp.float32),
            ],
        ),
        out_shape=[jax.ShapeDtypeStruct((n, 16, LATENT_WIDTH), jnp.bfloat16)] * (2 * N_X),
        compiler_params=pltpu.CompilerParams(vmem_limit_bytes=60 * 1024 * 1024),
        cost_estimate=pl.CostEstimate(
            flops=2 * n * heads * 256 * (width + LATENT_WIDTH),
            bytes_accessed=count * 800_000,
            transcendentals=n * heads * 256,
        ),
        name="attend",
    )(where, lengths, queries, cache, fresh)


def vmem_out(shape, dtype=jnp.bfloat16):
    return pltpu.VMEM(shape, dtype)


HBM_SPEC = pl.BlockSpec(memory_space=pltpu.HBM)
VMEM_SPEC = pl.BlockSpec(memory_space=pltpu.VMEM)


def run_copies(copies):
    for copy in copies:
        copy.start()
    for copy in copies:
        copy.wait()


def hold_projection_kernel(up_own, up_other, out_own, out_other, up_ref, out_ref, sems):
    half = out_own.shape[0]
    pairs = [
        (up_own, up_ref.at[0:8]),
        (up_other, up_ref.at[8:16]),
        (out_own, out_ref.at[0:half]),
        (out_other, out_ref.at[half : 2 * half]),
    ]
    run_copies([pltpu.make_async_copy(a, b, sems.at[i]) for i, (a, b) in enumerate(pairs)])


def hold_projection(up_own, up_other, out_own, out_other):
    return pl.pallas_call(
        hold_projection_kernel,
        in_specs=[HBM_SPEC] * 4,
        out_specs=[VMEM_SPEC] * 2,
        out_shape=[
            vmem_out((16,) + up_own.shape[1:]),
            vmem_out((2 * out_own.shape[0], out_own.shape[1])),
        ],
        scratch_shapes=[pltpu.SemaphoreType.DMA((4,))],
        cost_estimate=pl.CostEstimate(flops=0, bytes_accessed=17_000_000, transcendentals=0),
        compiler_params=pltpu.CompilerParams(vmem_limit_bytes=16 * 1024 * 1024),
        name="hold_projection",
    )(up_own, up_other, out_own, out_other)


def hold_feed_kernel(g0, g1, u0, u1, d0, d1, own_ref, other_ref, down_ref, sems):
    units = g0.shape[1]
    pairs = []
    for side, (g, u, d) in enumerate(((g0, u0, d0), (g1, u1, d1))):
        mix = (own_ref, other_ref)[side]
        for j in range(units // 128):
            cols = slice(j * 128, (j + 1) * 128)
            pairs.append((g.at[:, cols], mix.at[j, :, 0:128]))
            pairs.append((u.at[:, cols], mix.at[j, :, 128:256]))
        pairs.append((d, down_ref.at[side * units : (side + 1) * units]))
    run_copies([pltpu.make_async_copy(a, b, sems.at[i]) for i, (a, b) in enumerate(pairs)])


def hold_feed(g0, g1, u0, u1, d0, d1):
    width, units = g0.shape
    tiles = units // 128
    return pl.pallas_call(
        hold_feed_kernel,
        in_specs=[HBM_SPEC] * 6,
        out_specs=[VMEM_SPEC] * 3,
        out_shape=[vmem_out((tiles, width, 256))] * 2 + [vmem_out((2 * units, width))],
        scratch_shapes=[pltpu.SemaphoreType.DMA((4 * tiles + 2,))],
        cost_estimate=pl.CostEstimate(flops=0, bytes_accessed=27_500_000, transcendentals=0),
        compiler_params=pltpu.CompilerParams(vmem_limit_bytes=16 * 1024 * 1024),
        name="hold_feed",
    )(g0, g1, u0, u1, d0, d1)


def values_kernel(*refs, blocks):
    lat, up_ref, out_ref, turned = refs[:blocks], refs[blocks], refs[blocks + 1], refs[blocks + 2]
    heads, depth, wide = up_ref.shape
    n = lat[0].shape[0]
    for i, ref in enumerate(lat):

        @pl.loop(0, n)
        def _(r):
            row = ref[r].astype(jnp.float32)
            at = pl.multiple_of(i * n * heads + r * heads, heads)
            for lane in range(depth // 128):
                turned[lane, pl.ds(at, heads), :] = row[:, lane * 128 : (lane + 1) * 128]

    for h in range(heads):
        rows = jnp.concatenate(
            [turned[lane, pl.ds(h, blocks * n, stride=heads), :] for lane in range(depth // 128)],
            axis=1,
        ).astype(jnp.bfloat16)
        part = jnp.dot(rows, up_ref[h], preferred_element_type=jnp.float32)
        out_ref[:, h * wide : (h + 1) * wide] = part.astype(jnp.bfloat16)


def values_of(blocks, up):
    n, heads, depth = blocks[0].shape
    rows = n * len(blocks)
    wide = up.shape[2]
    return pl.pallas_call(
        functools.partial(values_kernel, blocks=len(blocks)),
        in_specs=[VMEM_SPEC] * (len(blocks) + 1),
        out_specs=VMEM_SPEC,
        out_shape=jax.ShapeDtypeStruct((rows, heads * wide), jnp.bfloat16),
        scratch_shapes=[pltpu.VMEM((depth // 128, rows * heads, 128), jnp.float32)],
        compiler_params=pltpu.CompilerParams(vmem_limit_bytes=16 * 1024 * 1024),
        cost_estimate=pl.CostEstimate(
            flops=2 * rows * heads * depth * wide, bytes_accessed=4_000_000, transcendentals=0
        ),
        name="values",
    )(*blocks, up)


def write_rows(part, outs, cols):
    at = 0
    for out in outs:
        size = out.shape[0]
        out[:, cols] = part[at : at + size].astype(out.dtype)
        at += size


def project_kernel(*refs, parts):
    count = len(parts)
    given, w_ref, outs, values = refs[:count], refs[count], refs[count + 1 : -1], refs[-1]
    at = 0
    for ref, (first, size) in zip(given, parts):
        values[at : at + size, :] = ref[first : first + size, :]
        at += size
    tile = 512

    @pl.loop(0, w_ref.shape[1] // tile)
    def _(j):
        cols = pl.ds(pl.multiple_of(j * tile, tile), tile)
        write_rows(
            jnp.dot(values[...], w_ref[:, cols], preferred_element_type=jnp.float32), outs, cols
        )


def project(values, out, shapes):
    parts = [(first, size) for _, first, size in values]
    rows = sum(size for _, size in parts)
    depth, width = out.shape
    return pl.pallas_call(
        functools.partial(project_kernel, parts=parts),
        in_specs=[VMEM_SPEC] * (len(values) + 1),
        out_specs=[VMEM_SPEC] * len(shapes),
        out_shape=[jax.ShapeDtypeStruct((r, width), d) for r, d in shapes],
        scratch_shapes=[pltpu.VMEM((rows, depth), jnp.bfloat16)],
        compiler_params=pltpu.CompilerParams(vmem_limit_bytes=16 * 1024 * 1024),
        cost_estimate=pl.CostEstimate(
            flops=2 * rows * depth * width, bytes_accessed=17_000_000, transcendentals=0
        ),
        name="project",
    )(*[v for v, _, _ in values], out)


def feed_kernel(*refs, blocks):
    given, mixes, down_ref = refs[:blocks], refs[blocks : blocks + 2], refs[blocks + 2]
    *outs, rows, hidden = refs[blocks + 3 :]
    at = 0
    for b in given:
        rows[at : at + b.shape[0], :] = b[...]
        at += b.shape[0]
    tiles = mixes[0].shape[0]
    for side, mix in enumerate(mixes):

        @pl.loop(0, tiles)
        def _(j):
            both = jnp.dot(rows[...], mix[j], preferred_element_type=jnp.float32)
            gate, up_part = both[:, :128], both[:, 128:]
            value = gate / (1.0 + jnp.exp(-gate)) * up_part
            at = pl.multiple_of((side * tiles + j) * 128, 128)
            hidden[:, pl.ds(at, 128)] = value.astype(jnp.bfloat16)

    tile = 512

    @pl.loop(0, down_ref.shape[1] // tile)
    def _(j):
        cols = pl.ds(pl.multiple_of(j * tile, tile), tile)
        write_rows(
            jnp.dot(hidden[...], down_ref[:, cols], preferred_element_type=jnp.float32), outs, cols
        )


def feed(blocks, held, shapes):
    rows = sum(b.shape[0] for b in blocks)
    units, width = held[2].shape
    return pl.pallas_call(
        functools.partial(feed_kernel, blocks=len(blocks)),
        in_specs=[VMEM_SPEC] * (len(blocks) + 3),
        out_specs=[VMEM_SPEC] * len(shapes),
        out_shape=[jax.ShapeDtypeStruct((r, width), d) for r, d in shapes],
        scratch_shapes=[
            pltpu.VMEM((rows, width), jnp.bfloat16),
            pltpu.VMEM((rows, units), jnp.bfloat16),
        ],
        compiler_params=pltpu.CompilerParams(vmem_limit_bytes=16 * 1024 * 1024),
        cost_estimate=pl.CostEstimate(
            flops=6 * rows * width * units, bytes_accessed=28_000_000, transcendentals=rows * units
        ),
        name="feed",
    )(*blocks, *held)


def after(value, *others):
    return lax.optimization_barrier((value,) + others)[0]


SMALL = pltpu.CompilerParams(vmem_limit_bytes=16 * 1024 * 1024)


def glue(kernel, name, args, shapes):
    return pl.pallas_call(
        kernel,
        in_specs=[VMEM_SPEC] * len(args),
        out_specs=[VMEM_SPEC] * len(shapes),
        out_shape=[jax.ShapeDtypeStruct(s, d) for s, d in shapes],
        compiler_params=SMALL,
        cost_estimate=pl.CostEstimate(flops=10_000, bytes_accessed=2_000_000, transcendentals=0),
        name=name,
    )(*args)


def flatten_kernel(hidden_ref, out_ref):
    steps = hidden_ref.shape[1]
    for r in range(hidden_ref.shape[0]):
        out_ref[r * steps : (r + 1) * steps, :] = hidden_ref[r].astype(jnp.float32)


def column_loop(width, body):
    tile = 512

    @pl.loop(0, width // tile)
    def _(j):
        body(pl.ds(pl.multiple_of(j * tile, tile), tile))


def fold_kernel(near_ref, back_ref, out_ref):
    def body(cols):
        total = near_ref[:, cols] + back_ref[:, cols].astype(jnp.float32)
        out_ref[:, cols] = total.astype(jnp.bfloat16)

    column_loop(near_ref.shape[1], body)


def fold(near, back):
    (out,) = glue(fold_kernel, "fold", (near, back), [(near.shape, jnp.bfloat16)])
    return out


def norm_kernel(hidden_ref, gain_ref, own_ref, *refs):
    *received, residual_ref, normed_ref, squares = refs
    width = own_ref.shape[1]
    squares[...] = jnp.zeros_like(squares)

    def add(cols):
        total = hidden_ref[:, cols] + own_ref[:, cols]
        for ref in received:
            total = total + ref[:, cols].astype(jnp.float32)
        residual_ref[:, cols] = total
        square = total * total
        for at in range(0, square.shape[1], 128):
            squares[...] += square[:, at : at + 128]

    column_loop(width, add)
    mean = jnp.sum(squares[...], axis=1, keepdims=True) / width
    scale = lax.rsqrt(mean + norm_eps)

    def write(cols):
        normed_ref[:, cols] = (residual_ref[:, cols] * scale * gain_ref[:, cols]).astype(jnp.bfloat16)

    column_loop(width, write)


def norm(own, received, hidden, gain):
    n, width = own.shape
    return pl.pallas_call(
        norm_kernel,
        in_specs=[VMEM_SPEC] * (3 + len(received)),
        out_specs=[VMEM_SPEC] * 2,
        out_shape=[
            jax.ShapeDtypeStruct((n, width), jnp.float32),
            jax.ShapeDtypeStruct((n, width), jnp.bfloat16),
        ],
        scratch_shapes=[pltpu.VMEM((n, 128), jnp.float32)],
        compiler_params=SMALL,
        cost_estimate=pl.CostEstimate(flops=10_000, bytes_accessed=2_000_000, transcendentals=0),
        name="norm",
    )(hidden, gain, own, *received)


def finish_kernel(residual_ref, own_ref, *refs):
    *received, out_ref = refs

    def body(cols):
        total = residual_ref[:, cols] + own_ref[:, cols]
        for ref in received:
            total = total + ref[:, cols].astype(jnp.float32)
        out_ref[:, cols] = total.astype(jnp.bfloat16)

    column_loop(own_ref.shape[1], body)


def page_kernel(ids_ref, partner_ref, request_ref, count_ref, cache_ref, block_ref, offset_ref):
    dp = ids_ref[3]
    offset_ref[0] = jnp.bitwise_xor(partner_ref[dp], dp)
    for k in range(MIG_MAX):
        rows = cache_ref[0, k * PAGE : (k + 1) * PAGE, :]
        block_ref[k] = jnp.where(k < count_ref[0], rows, jnp.zeros_like(rows))


def page_block(ids, partner, moved_request, moved_pages, cache):
    width = cache.shape[2]
    return pl.pallas_call(
        page_kernel,
        grid_spec=pltpu.PrefetchScalarGridSpec(
            num_scalar_prefetch=4,
            grid=(1,),
            in_specs=[pl.BlockSpec((1,) + cache.shape[1:], lambda i, ids, p, r, c: (r[0], 0, 0))],
            out_specs=[
                pl.BlockSpec((MIG_MAX, PAGE, width), lambda i, ids, p, r, c: (0, 0, 0)),
                pl.BlockSpec(memory_space=pltpu.SMEM),
            ],
        ),
        out_shape=[
            jax.ShapeDtypeStruct((MIG_MAX, PAGE, width), cache.dtype),
            jax.ShapeDtypeStruct((1,), jnp.int32),
        ],
        compiler_params=SMALL,
        cost_estimate=pl.CostEstimate(flops=1_000, bytes_accessed=400_000, transcendentals=0),
        name="pages",
    )(ids, partner.reshape(-1), moved_request, moved_pages, cache)


def pick_kernel(offset_ref, mine_ref, other_ref, out_ref, *, bit):
    trade = lax.rem(offset_ref[0] // (1 << bit), 2) == 1

    @pl.when(trade)
    def _():
        out_ref[...] = other_ref[...]

    @pl.when(jnp.logical_not(trade))
    def _():
        out_ref[...] = mine_ref[...]


def page_step(block, offset, bit):
    other = lax.ppermute(block, "dp", [(d, d ^ (1 << bit)) for d in range(8)])
    return pl.pallas_call(
        functools.partial(pick_kernel, bit=bit),
        in_specs=[pl.BlockSpec(memory_space=pltpu.SMEM), VMEM_SPEC, VMEM_SPEC],
        out_specs=VMEM_SPEC,
        out_shape=jax.ShapeDtypeStruct(block.shape, block.dtype),
        compiler_params=SMALL,
        cost_estimate=pl.CostEstimate(flops=1_000, bytes_accessed=400_000, transcendentals=0),
        name="pick",
    )(offset, block, other)


def local(
    request_latent_cache,
    lengths,
    queries,
    incoming_keys,
    hidden_in,
    value_up_weight,
    w_out,
    norm_gain,
    w_gate,
    w_up,
    w_down,
    partner,
    moved_request,
    moved_pages,
):
    req_here, steps_here, width = hidden_in.shape
    n = req_here * steps_here
    t = lax.axis_index("tp")
    where = jnp.stack([t // 8, (t // 2) % N_X, t % 2, lax.axis_index("dp")])
    up_other, out_other, gate_other = swap_cores(value_up_weight), swap_cores(w_out), swap_cores(w_gate)
    turned = jnp.swapaxes(queries, 2, 3)
    own0, own1, own2, own3, go0, go1, go2, go3 = attend(
        where, lengths, turned, request_latent_cache, incoming_keys, 0, req_here
    )
    near_shapes = [(n, jnp.float32), (n, jnp.float32), (n, jnp.bfloat16), (n, jnp.float32)]
    far_shapes = [(n, jnp.bfloat16)] * N_X

    go1, go3, own2 = after(go1, up_other), after(go3, up_other), after(own2, up_other)
    far_in1, far_in3 = shift(go1, dz=1), shift(go3, dz=-1)
    near2 = shift(own2, dx=2)
    first = (near2, far_in1, far_in3, out_other, gate_other)
    far1 = shift(after(far_in1, *first), dx=1)
    far3 = shift(after(far_in3, *first), dx=3)
    far_in2, far_in0 = shift(after(go2, *first), dz=-1), shift(after(go0, *first), dz=1)
    far2 = shift(far_in2, dx=2)
    near1 = shift(after(own1, far_in0, far_in2), dx=1)
    near3 = shift(after(own3, far_in0, far_in2), dx=3)
    up2, out2 = hold_projection(value_up_weight, up_other, w_out, out_other)
    second = (far_in0, far_in2, far1, far3)
    fup_other = swap_cores(after(w_up, *second))
    down_other = swap_cores(after(w_down, *second))
    block, offset = page_block(
        after(where, *first), partner, moved_request, moved_pages, request_latent_cache
    )
    (hidden32,) = glue(
        flatten_kernel, "flatten", (after(hidden_in, *first),), [((n, width), jnp.float32)]
    )
    gain = norm_gain.reshape(1, width)
    values_a = values_of([after(own0, near2), near2], up2)
    values_b = values_of([far_in0, far1], up2)
    values_c = values_of([far2, far3], up2)
    far = project(
        [(values_b, 0, 2 * n), (values_c, 0, 2 * n)], out2, far_shapes
    )
    back1, back3 = shift(far[1], dz=-1), shift(far[3], dz=1)
    aside, back0 = shift(far[2], dx=-2), shift(far[0], dz=-1)
    values_d = values_of([after(near1, far[0]), near3], up2)
    near = project(
        [(values_a, 0, n), (values_d, 0, n), (values_a, n, n), (values_d, n, n)], out2, near_shapes
    )
    home2 = shift(near[2], dx=-2)
    back2 = shift(aside, dz=1)
    fold1, fold3 = fold(near[1], back1), fold(near[3], back3)
    home1, home3 = shift(fold1, dx=-1), shift(fold3, dx=-3)
    held = hold_feed(after(w_gate, fold1, fold3), gate_other, w_up, fup_other, w_down, down_other)
    residual, normed = norm(
        near[0], [back0, back2, after(home1, held[0]), home2, home3], hidden32, gain
    )

    row1, row3 = shift(normed, dx=1), shift(normed, dx=3)
    over, under = shift(normed, dz=1), shift(normed, dz=-1)
    row2 = shift(normed, dx=2)
    far_row1, far_row3 = shift(row1, dz=1), shift(row3, dz=-1)
    far_row2 = shift(under, dx=2)
    block = page_step(after(block, normed), offset, 0)
    near = feed([normed, row1, row2, row3], held, near_shapes)
    home2 = shift(near[2], dx=-2)
    far = feed([after(over, near[0]), far_row1, far_row2, far_row3], held, far_shapes)
    back1, back3 = shift(far[1], dz=-1), shift(far[3], dz=1)
    aside, back0 = shift(far[2], dx=-2), shift(far[0], dz=-1)
    block = page_step(after(block, far[0]), offset, 1)
    fold1, fold3 = fold(near[1], back1), fold(near[3], back3)
    home1, home3 = shift(fold1, dx=-1), shift(fold3, dx=-3)
    back2 = shift(aside, dz=1)
    block = page_step(after(block, fold1), offset, 2)
    (out,) = glue(
        finish_kernel, "finish", (residual, near[0], back0, back2, home1, home2, home3),
        [((n, width), jnp.bfloat16)],
    )
    return out.reshape(req_here, steps_here, width), block


def solution(mesh):
    in_specs = (
        P(("dp", "tp"), None, None),
        P(("dp", "tp")),
        P(("dp", "tp"), None, None, None),
        P(("dp", "tp"), None, None),
        P(("dp", "tp"), None, None),
        P("tp", None, None),
        P("tp", None),
        P(),
        P(None, "tp"),
        P(None, "tp"),
        P("tp", None),
        P(None, "tp"),
        P(("dp", "tp")),
        P(("dp", "tp")),
    )
    out_specs = (P(("dp", "tp"), None, None), P(("dp", "tp"), None, None))
    return jax.shard_map(local, mesh=mesh, in_specs=in_specs, out_specs=out_specs, check_vma=False)
```

```python
import functools

import jax
import jax.numpy as jnp
from jax import lax
from jax.experimental import pallas as pl
from jax.experimental.pallas import tpu as pltpu
from jax.sharding import PartitionSpec as P

LATENT_WIDTH = 512
PAGE = 64
MIG_MAX = 2
N_X = 4
N_Z = 4
N_Y = 4
GRID = ("dp", "tp")
T_PAD = 208
GROUP = 4

score_scale = 192.0 ** (-0.5)
masked_score = -1e30
norm_eps = 1e-06


def place(index):
    d, t = index // 16, index % 16
    return (d // 4) * 2 + t // 8, d % 4, (t // 2) % 4, t % 2


def index_of(z, y, x, c):
    z, y, x = z % N_Z, y % N_Y, x % N_X
    return ((z // 2) * 4 + y) * 16 + (z % 2) * 8 + x * 2 + c


def shift(value, dx=0, dz=0):
    pairs = []
    for i in range(128):
        z, y, x, c = place(i)
        pairs.append((i, index_of(z + dz, y, x + dx, c)))
    return lax.ppermute(value, GRID, pairs)


def swap_cores(value):
    return lax.ppermute(value, "tp", [(t, t ^ 1) for t in range(16)])


def attend_kernel(where_ref, lens_ref, q_ref, cache_ref, fresh_ref, *rest, first_request):
    *outs, keys, rows = rest
    i = pl.program_id(0)
    reqs, steps, width, heads = q_ref.shape
    capacity = cache_ref.shape[1]
    total = keys.shape[1]

    @pl.when(i == 0)
    def _():
        keys[...] = jnp.zeros_like(keys)

    position = lax.broadcasted_iota(jnp.int32, (total, steps * heads), 0)
    column = lax.broadcasted_iota(jnp.int32, (total, steps * heads), 1)
    fresh_ok = (position >= capacity) & (position - capacity <= column // heads)
    z, x, c = where_ref[0], where_ref[1], where_ref[2]
    group = keys.shape[0]
    for first in range(0, reqs, group):
        scores, probs = [], []
        for g in range(group):
            r = first + g
            keys[g, 0:capacity, :] = cache_ref[r]
            keys[g, capacity : capacity + steps, :] = fresh_ref[r]
            q = jnp.concatenate([q_ref[r, s] for s in range(steps)], axis=1)
            scores.append(jnp.dot(keys[g], q, preferred_element_type=jnp.float32))
        for g in range(group):
            visible = (position < lens_ref[first_request + i * reqs + first + g]) | fresh_ok
            masked = jnp.where(visible, scores[g] * score_scale, masked_score)
            peak = jnp.max(masked, axis=0, keepdims=True)
            weight = jnp.exp(masked - peak)
            inverse = 1.0 / jnp.sum(weight, axis=0, keepdims=True)
            probs.append((weight * inverse).astype(jnp.bfloat16))
        for g in range(group):
            latent = lax.dot_general(
                probs[g],
                keys[g, :, :LATENT_WIDTH],
                (((0,), (0,)), ((), ())),
                preferred_element_type=jnp.float32,
            )
            rows[g] = latent
        for g in range(group):
            at = (i * reqs + first + g) * steps
            for side in range(2):
                zz = z if side == 0 else 1 - z
                for rel in range(N_X):
                    out = outs[side * N_X + rel]
                    chip = zz * 64 + lax.rem(x + rel, N_X) * 16
                    for s in range(steps):
                        picked = [
                            rows[g, pl.ds(pl.multiple_of(s * heads + chip + core * 8, 8), 8), :]
                            for core in (c, 1 - c)
                        ]
                        out[at + s] = jnp.concatenate(picked, axis=0).astype(jnp.bfloat16)


def attend(where, lengths, queries, cache, fresh, first, count):
    reqs, steps, width, heads = queries.shape
    capacity = cache.shape[1]
    part = 4
    n = count * steps
    base = first // part
    return pl.pallas_call(
        functools.partial(attend_kernel, first_request=first),
        grid_spec=pltpu.PrefetchScalarGridSpec(
            num_scalar_prefetch=2,
            grid=(count // part,),
            in_specs=[
                pl.BlockSpec((part, steps, width, heads), lambda i, w, l: (base + i, 0, 0, 0)),
                pl.BlockSpec((part, capacity, width), lambda i, w, l: (base + i, 0, 0)),
                pl.BlockSpec((part, steps, width), lambda i, w, l: (base + i, 0, 0)),
            ],
            out_specs=[pl.BlockSpec((n, 16, LATENT_WIDTH), lambda i, w, l: (0, 0, 0))] * (2 * N_X),
            scratch_shapes=[
                pltpu.VMEM((GROUP, T_PAD, width), jnp.bfloat16),
                pltpu.VMEM((GROUP, steps * heads, LATENT_WIDTH), jnp.float32),
            ],
        ),
        out_shape=[jax.ShapeDtypeStruct((n, 16, LATENT_WIDTH), jnp.bfloat16)] * (2 * N_X),
        compiler_params=pltpu.CompilerParams(vmem_limit_bytes=60 * 1024 * 1024),
        cost_estimate=pl.CostEstimate(
            flops=2 * n * heads * 256 * (width + LATENT_WIDTH),
            bytes_accessed=count * 800_000,
            transcendentals=n * heads * 256,
        ),
        name="attend",
    )(where, lengths, queries, cache, fresh)


def vmem_out(shape, dtype=jnp.bfloat16):
    return pltpu.VMEM(shape, dtype)


HBM_SPEC = pl.BlockSpec(memory_space=pltpu.HBM)
ANY_SPEC = pl.BlockSpec(memory_space=pl.ANY)
VMEM_SPEC = pl.BlockSpec(memory_space=pltpu.VMEM)


def in_hbm(value):
    return pltpu.with_memory_space_constraint(value, pltpu.HBM)


def run_copies(copies):
    for copy in copies:
        copy.start()
    for copy in copies:
        copy.wait()


def hold_projection_kernel(up_own, up_other, out_own, out_other, up_ref, out_ref, sems):
    half = out_own.shape[0]
    pairs = [
        (up_own, up_ref.at[0:8]),
        (up_other, up_ref.at[8:16]),
        (out_own, out_ref.at[0:half]),
        (out_other, out_ref.at[half : 2 * half]),
    ]
    run_copies([pltpu.make_async_copy(a, b, sems.at[i]) for i, (a, b) in enumerate(pairs)])


def hold_projection(up_own, up_other, out_own, out_other):
    return pl.pallas_call(
        hold_projection_kernel,
        in_specs=[HBM_SPEC, ANY_SPEC] * 2,
        out_specs=[VMEM_SPEC] * 2,
        out_shape=[
            vmem_out((16,) + up_own.shape[1:]),
            vmem_out((2 * out_own.shape[0], out_own.shape[1])),
        ],
        scratch_shapes=[pltpu.SemaphoreType.DMA((4,))],
        cost_estimate=pl.CostEstimate(flops=0, bytes_accessed=17_000_000, transcendentals=0),
        compiler_params=pltpu.CompilerParams(vmem_limit_bytes=16 * 1024 * 1024),
        name="hold_projection",
    )(in_hbm(up_own), up_other, in_hbm(out_own), out_other)


def hold_feed_kernel(g0, g1, u0, u1, d0, d1, own_ref, other_ref, down_ref, sems):
    units = g0.shape[1]
    pairs = []
    for side, (g, u, d) in enumerate(((g0, u0, d0), (g1, u1, d1))):
        mix = (own_ref, other_ref)[side]
        for j in range(units // 128):
            cols = slice(j * 128, (j + 1) * 128)
            pairs.append((g.at[:, cols], mix.at[j, :, 0:128]))
            pairs.append((u.at[:, cols], mix.at[j, :, 128:256]))
        pairs.append((d, down_ref.at[side * units : (side + 1) * units]))
    run_copies([pltpu.make_async_copy(a, b, sems.at[i]) for i, (a, b) in enumerate(pairs)])


def hold_feed(g0, g1, u0, u1, d0, d1):
    width, units = g0.shape
    tiles = units // 128
    return pl.pallas_call(
        hold_feed_kernel,
        in_specs=[HBM_SPEC, ANY_SPEC] * 3,
        out_specs=[VMEM_SPEC] * 3,
        out_shape=[vmem_out((tiles, width, 256))] * 2 + [vmem_out((2 * units, width))],
        scratch_shapes=[pltpu.SemaphoreType.DMA((4 * tiles + 2,))],
        cost_estimate=pl.CostEstimate(flops=0, bytes_accessed=27_500_000, transcendentals=0),
        compiler_params=pltpu.CompilerParams(vmem_limit_bytes=16 * 1024 * 1024),
        name="hold_feed",
    )(in_hbm(g0), g1, in_hbm(u0), u1, in_hbm(d0), d1)


def values_kernel(*refs, blocks):
    lat, up_ref, out_ref, turned = refs[:blocks], refs[blocks], refs[blocks + 1], refs[blocks + 2]
    heads, depth, wide = up_ref.shape
    n = lat[0].shape[0]
    for i, ref in enumerate(lat):

        @pl.loop(0, n)
        def _(r):
            row = ref[r].astype(jnp.float32)
            at = pl.multiple_of(i * n * heads + r * heads, heads)
            for lane in range(depth // 128):
                turned[lane, pl.ds(at, heads), :] = row[:, lane * 128 : (lane + 1) * 128]

    for h in range(heads):
        rows = jnp.concatenate(
            [turned[lane, pl.ds(h, blocks * n, stride=heads), :] for lane in range(depth // 128)],
            axis=1,
        ).astype(jnp.bfloat16)
        part = jnp.dot(rows, up_ref[h], preferred_element_type=jnp.float32)
        out_ref[:, h * wide : (h + 1) * wide] = part.astype(jnp.bfloat16)


def values_of(blocks, up):
    n, heads, depth = blocks[0].shape
    rows = n * len(blocks)
    wide = up.shape[2]
    return pl.pallas_call(
        functools.partial(values_kernel, blocks=len(blocks)),
        in_specs=[VMEM_SPEC] * (len(blocks) + 1),
        out_specs=VMEM_SPEC,
        out_shape=jax.ShapeDtypeStruct((rows, heads * wide), jnp.bfloat16),
        scratch_shapes=[pltpu.VMEM((depth // 128, rows * heads, 128), jnp.float32)],
        compiler_params=pltpu.CompilerParams(vmem_limit_bytes=16 * 1024 * 1024),
        cost_estimate=pl.CostEstimate(
            flops=2 * rows * heads * depth * wide, bytes_accessed=4_000_000, transcendentals=0
        ),
        name="values",
    )(*blocks, up)


def write_rows(part, outs, cols):
    at = 0
    for out in outs:
        size = out.shape[0]
        out[:, cols] = part[at : at + size].astype(out.dtype)
        at += size


def project_kernel(*refs, parts):
    count = len(parts)
    given, w_ref, outs, values = refs[:count], refs[count], refs[count + 1 : -1], refs[-1]
    at = 0
    for ref, (first, size) in zip(given, parts):
        values[at : at + size, :] = ref[first : first + size, :]
        at += size
    tile = 512

    @pl.loop(0, w_ref.shape[1] // tile)
    def _(j):
        cols = pl.ds(pl.multiple_of(j * tile, tile), tile)
        write_rows(
            jnp.dot(values[...], w_ref[:, cols], preferred_element_type=jnp.float32), outs, cols
        )


def project(values, out, shapes):
    parts = [(first, size) for _, first, size in values]
    rows = sum(size for _, size in parts)
    depth, width = out.shape
    return pl.pallas_call(
        functools.partial(project_kernel, parts=parts),
        in_specs=[VMEM_SPEC] * (len(values) + 1),
        out_specs=[VMEM_SPEC] * len(shapes),
        out_shape=[jax.ShapeDtypeStruct((r, width), d) for r, d in shapes],
        scratch_shapes=[pltpu.VMEM((rows, depth), jnp.bfloat16)],
        compiler_params=pltpu.CompilerParams(vmem_limit_bytes=16 * 1024 * 1024),
        cost_estimate=pl.CostEstimate(
            flops=2 * rows * depth * width, bytes_accessed=17_000_000, transcendentals=0
        ),
        name="project",
    )(*[v for v, _, _ in values], out)


def feed_kernel(*refs, blocks):
    given, mixes, down_ref = refs[:blocks], refs[blocks : blocks + 2], refs[blocks + 2]
    *outs, rows, hidden = refs[blocks + 3 :]
    at = 0
    for b in given:
        rows[at : at + b.shape[0], :] = b[...]
        at += b.shape[0]
    tiles = mixes[0].shape[0]
    for side, mix in enumerate(mixes):

        @pl.loop(0, tiles)
        def _(j):
            both = jnp.dot(rows[...], mix[j], preferred_element_type=jnp.float32)
            gate, up_part = both[:, :128], both[:, 128:]
            value = gate / (1.0 + jnp.exp(-gate)) * up_part
            at = pl.multiple_of((side * tiles + j) * 128, 128)
            hidden[:, pl.ds(at, 128)] = value.astype(jnp.bfloat16)

    tile = 512

    @pl.loop(0, down_ref.shape[1] // tile)
    def _(j):
        cols = pl.ds(pl.multiple_of(j * tile, tile), tile)
        write_rows(
            jnp.dot(hidden[...], down_ref[:, cols], preferred_element_type=jnp.float32), outs, cols
        )


def feed(blocks, held, shapes):
    rows = sum(b.shape[0] for b in blocks)
    units, width = held[2].shape
    return pl.pallas_call(
        functools.partial(feed_kernel, blocks=len(blocks)),
        in_specs=[VMEM_SPEC] * (len(blocks) + 3),
        out_specs=[VMEM_SPEC] * len(shapes),
        out_shape=[jax.ShapeDtypeStruct((r, width), d) for r, d in shapes],
        scratch_shapes=[
            pltpu.VMEM((rows, width), jnp.bfloat16),
            pltpu.VMEM((rows, units), jnp.bfloat16),
        ],
        compiler_params=pltpu.CompilerParams(vmem_limit_bytes=16 * 1024 * 1024),
        cost_estimate=pl.CostEstimate(
            flops=6 * rows * width * units, bytes_accessed=28_000_000, transcendentals=rows * units
        ),
        name="feed",
    )(*blocks, *held)


def after(value, *others):
    return lax.optimization_barrier((value,) + others)[0]


SMALL = pltpu.CompilerParams(vmem_limit_bytes=16 * 1024 * 1024)


def glue(kernel, name, args, shapes):
    return pl.pallas_call(
        kernel,
        in_specs=[VMEM_SPEC] * len(args),
        out_specs=[VMEM_SPEC] * len(shapes),
        out_shape=[jax.ShapeDtypeStruct(s, d) for s, d in shapes],
        compiler_params=SMALL,
        cost_estimate=pl.CostEstimate(flops=10_000, bytes_accessed=2_000_000, transcendentals=0),
        name=name,
    )(*args)


def flatten_kernel(hidden_ref, out_ref):
    steps = hidden_ref.shape[1]
    for r in range(hidden_ref.shape[0]):
        out_ref[r * steps : (r + 1) * steps, :] = hidden_ref[r].astype(jnp.float32)


def column_loop(width, body):
    tile = 512

    @pl.loop(0, width // tile)
    def _(j):
        body(pl.ds(pl.multiple_of(j * tile, tile), tile))


def fold_kernel(near_ref, back_ref, out_ref):
    def body(cols):
        total = near_ref[:, cols] + back_ref[:, cols].astype(jnp.float32)
        out_ref[:, cols] = total.astype(jnp.bfloat16)

    column_loop(near_ref.shape[1], body)


def fold(near, back):
    (out,) = glue(fold_kernel, "fold", (near, back), [(near.shape, jnp.bfloat16)])
    return out


def norm_kernel(hidden_ref, gain_ref, own_ref, *refs):
    *received, residual_ref, normed_ref, squares = refs
    width = own_ref.shape[1]
    squares[...] = jnp.zeros_like(squares)

    def add(cols):
        total = hidden_ref[:, cols] + own_ref[:, cols]
        for ref in received:
            total = total + ref[:, cols].astype(jnp.float32)
        residual_ref[:, cols] = total
        square = total * total
        for at in range(0, square.shape[1], 128):
            squares[...] += square[:, at : at + 128]

    column_loop(width, add)
    mean = jnp.sum(squares[...], axis=1, keepdims=True) / width
    scale = lax.rsqrt(mean + norm_eps)

    def write(cols):
        normed_ref[:, cols] = (residual_ref[:, cols] * scale * gain_ref[:, cols]).astype(jnp.bfloat16)

    column_loop(width, write)


def norm(own, received, hidden, gain):
    n, width = own.shape
    return pl.pallas_call(
        norm_kernel,
        in_specs=[VMEM_SPEC] * (3 + len(received)),
        out_specs=[VMEM_SPEC] * 2,
        out_shape=[
            jax.ShapeDtypeStruct((n, width), jnp.float32),
            jax.ShapeDtypeStruct((n, width), jnp.bfloat16),
        ],
        scratch_shapes=[pltpu.VMEM((n, 128), jnp.float32)],
        compiler_params=SMALL,
        cost_estimate=pl.CostEstimate(flops=10_000, bytes_accessed=2_000_000, transcendentals=0),
        name="norm",
    )(hidden, gain, own, *received)


def finish_kernel(residual_ref, own_ref, *refs):
    *received, out_ref = refs

    def body(cols):
        total = residual_ref[:, cols] + own_ref[:, cols]
        for ref in received:
            total = total + ref[:, cols].astype(jnp.float32)
        out_ref[:, cols] = total.astype(jnp.bfloat16)

    column_loop(own_ref.shape[1], body)


def page_kernel(ids_ref, partner_ref, request_ref, count_ref, cache_ref, block_ref, offset_ref):
    dp = ids_ref[3]
    offset_ref[0] = jnp.bitwise_xor(partner_ref[dp], dp)
    for k in range(MIG_MAX):
        rows = cache_ref[0, k * PAGE : (k + 1) * PAGE, :]
        block_ref[k] = jnp.where(k < count_ref[0], rows, jnp.zeros_like(rows))


def page_block(ids, partner, moved_request, moved_pages, cache):
    width = cache.shape[2]
    return pl.pallas_call(
        page_kernel,
        grid_spec=pltpu.PrefetchScalarGridSpec(
            num_scalar_prefetch=4,
            grid=(1,),
            in_specs=[pl.BlockSpec((1,) + cache.shape[1:], lambda i, ids, p, r, c: (r[0], 0, 0))],
            out_specs=[
                pl.BlockSpec((MIG_MAX, PAGE, width), lambda i, ids, p, r, c: (0, 0, 0)),
                pl.BlockSpec(memory_space=pltpu.SMEM),
            ],
        ),
        out_shape=[
            jax.ShapeDtypeStruct((MIG_MAX, PAGE, width), cache.dtype),
            jax.ShapeDtypeStruct((1,), jnp.int32),
        ],
        compiler_params=SMALL,
        cost_estimate=pl.CostEstimate(flops=1_000, bytes_accessed=400_000, transcendentals=0),
        name="pages",
    )(ids, partner.reshape(-1), moved_request, moved_pages, in_hbm(cache))


def pick_kernel(offset_ref, mine_ref, other_ref, out_ref, *, bit):
    trade = lax.rem(offset_ref[0] // (1 << bit), 2) == 1

    @pl.when(trade)
    def _():
        out_ref[...] = other_ref[...]

    @pl.when(jnp.logical_not(trade))
    def _():
        out_ref[...] = mine_ref[...]


def page_trade(block, bit):
    return lax.ppermute(block, "dp", [(d, d ^ (1 << bit)) for d in range(8)])


def page_pick(block, other, offset, bit):
    return pl.pallas_call(
        functools.partial(pick_kernel, bit=bit),
        in_specs=[pl.BlockSpec(memory_space=pltpu.SMEM), VMEM_SPEC, VMEM_SPEC],
        out_specs=VMEM_SPEC,
        out_shape=jax.ShapeDtypeStruct(block.shape, block.dtype),
        compiler_params=SMALL,
        cost_estimate=pl.CostEstimate(flops=1_000, bytes_accessed=400_000, transcendentals=0),
        name="pick",
    )(offset, block, other)


def local(
    request_latent_cache,
    lengths,
    queries,
    incoming_keys,
    hidden_in,
    value_up_weight,
    w_out,
    norm_gain,
    w_gate,
    w_up,
    w_down,
    partner,
    moved_request,
    moved_pages,
):
    req_here, steps_here, width = hidden_in.shape
    n = req_here * steps_here
    t = lax.axis_index("tp")
    where = jnp.stack([t // 8, (t // 2) % N_X, t % 2, lax.axis_index("dp")])
    up_other, out_other, gate_other = swap_cores(value_up_weight), swap_cores(w_out), swap_cores(w_gate)
    turned = jnp.swapaxes(queries, 2, 3)
    own0, own1, own2, own3, go0, go1, go2, go3 = attend(
        where, lengths, turned, request_latent_cache, incoming_keys, 0, req_here
    )
    near_shapes = [(n, jnp.float32), (n, jnp.float32), (n, jnp.bfloat16), (n, jnp.float32)]
    far_shapes = [(n, jnp.bfloat16)] * N_X

    go1, go3, own2 = after(go1, up_other), after(go3, up_other), after(own2, up_other)
    far_in1, far_in3 = shift(go1, dz=1), shift(go3, dz=-1)
    near2 = shift(own2, dx=2)
    block, offset = page_block(
        after(where, go1), partner, moved_request, moved_pages, request_latent_cache
    )
    traded = page_trade(block, 0)
    first = (near2, far_in1, far_in3, out_other, gate_other)
    far1 = shift(after(far_in1, *first), dx=1)
    far3 = shift(after(far_in3, *first), dx=3)
    far_in2, far_in0 = shift(after(go2, *first), dz=-1), shift(after(go0, *first), dz=1)
    far2 = shift(far_in2, dx=2)
    near1 = shift(after(own1, far_in0, far_in2), dx=1)
    near3 = shift(after(own3, far_in0, far_in2), dx=3)
    up2, out2 = hold_projection(value_up_weight, up_other, w_out, out_other)
    block = page_pick(block, after(traded, *first), offset, 0)
    traded = page_trade(block, 1)
    second = (far_in0, far_in2, far1, far3, block)
    fup_other = swap_cores(after(w_up, *second))
    down_other = swap_cores(after(w_down, *second))
    (hidden32,) = glue(
        flatten_kernel, "flatten", (after(hidden_in, *first),), [((n, width), jnp.float32)]
    )
    gain = norm_gain.reshape(1, width)
    values_a = values_of([after(own0, near2), near2], up2)
    values_b = values_of([far_in0, far1], up2)
    values_c = values_of([far2, far3], up2)
    block = page_pick(block, after(traded, far2), offset, 1)
    values_b = after(values_b, values_a, block)
    far = project([(values_b, 0, 2 * n), (values_c, 0, 2 * n)], out2, far_shapes)
    back1, back3 = shift(far[1], dz=-1), shift(far[3], dz=1)
    aside, back0 = shift(far[2], dx=-2), shift(far[0], dz=-1)
    values_d = values_of([after(near1, far[0]), near3], up2)
    near = project(
        [(values_a, 0, n), (values_d, 0, n), (values_a, n, n), (values_d, n, n)], out2, near_shapes
    )
    home2 = shift(near[2], dx=-2)
    back2 = shift(aside, dz=1)
    fold1, fold3 = fold(near[1], back1), fold(near[3], back3)
    home1, home3 = shift(fold1, dx=-1), shift(fold3, dx=-3)
    held = hold_feed(after(w_gate, fold1, fold3), gate_other, w_up, fup_other, w_down, down_other)
    residual, normed = norm(
        near[0], [back0, back2, after(home1, held[0]), home2, home3], hidden32, gain
    )

    row1, row3 = shift(normed, dx=1), shift(normed, dx=3)
    over, under = shift(normed, dz=1), shift(normed, dz=-1)
    row2 = shift(normed, dx=2)
    traded = page_trade(after(block, normed), 2)
    far_row1, far_row3 = shift(row1, dz=1), shift(row3, dz=-1)
    far_row2 = shift(under, dx=2)
    near = feed([normed, row1, row2, row3], held, near_shapes)
    home2 = shift(near[2], dx=-2)
    block = page_pick(block, after(traded, near[0]), offset, 2)
    far = feed([after(over, near[0], block), far_row1, far_row2, far_row3], held, far_shapes)
    back1, back3 = shift(far[1], dz=-1), shift(far[3], dz=1)
    aside, back0 = shift(far[2], dx=-2), shift(far[0], dz=-1)
    fold1, fold3 = fold(near[1], back1), fold(near[3], back3)
    home1, home3 = shift(fold1, dx=-1), shift(fold3, dx=-3)
    back2 = shift(aside, dz=1)
    (out,) = glue(
        finish_kernel, "finish", (residual, near[0], back0, back2, home1, home2, home3),
        [((n, width), jnp.bfloat16)],
    )
    return out.reshape(req_here, steps_here, width), block


def solution(mesh):
    in_specs = (
        P(("dp", "tp"), None, None),
        P(("dp", "tp")),
        P(("dp", "tp"), None, None, None),
        P(("dp", "tp"), None, None),
        P(("dp", "tp"), None, None),
        P("tp", None, None),
        P("tp", None),
        P(),
        P(None, "tp"),
        P(None, "tp"),
        P("tp", None),
        P(None, "tp"),
        P(("dp", "tp")),
        P(("dp", "tp")),
    )
    out_specs = (P(("dp", "tp"), None, None), P(("dp", "tp"), None, None))
    return jax.shard_map(local, mesh=mesh, in_specs=in_specs, out_specs=out_specs, check_vma=False)
```

```python
import functools

import jax
import jax.numpy as jnp
from jax import lax
from jax.experimental import pallas as pl
from jax.experimental.pallas import tpu as pltpu
from jax.sharding import PartitionSpec as P

LATENT_WIDTH = 512
PAGE = 64
MIG_MAX = 2
N_X = 4
N_Z = 4
N_Y = 4
GRID = ("dp", "tp")
T_PAD = 208
GROUP = 8

score_scale = 192.0 ** (-0.5)
masked_score = -1e30
norm_eps = 1e-06


def place(index):
    d, t = index // 16, index % 16
    return (d // 4) * 2 + t // 8, d % 4, (t // 2) % 4, t % 2


def index_of(z, y, x, c):
    z, y, x = z % N_Z, y % N_Y, x % N_X
    return ((z // 2) * 4 + y) * 16 + (z % 2) * 8 + x * 2 + c


def shift(value, dx=0, dz=0):
    pairs = []
    for i in range(128):
        z, y, x, c = place(i)
        pairs.append((i, index_of(z + dz, y, x + dx, c)))
    return lax.ppermute(value, GRID, pairs)


def swap_cores(value):
    return lax.ppermute(value, "tp", [(t, t ^ 1) for t in range(16)])


def attend_kernel(lens_ref, q_ref, cache_ref, fresh_ref, *rest, first_request):
    *outs, keys, rows = rest
    i = pl.program_id(0)
    reqs, steps, width, heads = q_ref.shape
    capacity = cache_ref.shape[1]
    total = keys.shape[1]

    @pl.when(i == 0)
    def _():
        keys[...] = jnp.zeros_like(keys)

    position = lax.broadcasted_iota(jnp.int32, (total, steps * heads), 0)
    column = lax.broadcasted_iota(jnp.int32, (total, steps * heads), 1)
    fresh_ok = (position >= capacity) & (position - capacity <= column // heads)
    t = lax.axis_index("tp")
    z, x, c = t // 8, lax.rem(t // 2, N_X), lax.rem(t, 2)
    group = keys.shape[0]
    for first in range(0, reqs, group):
        scores, probs = [], []
        for g in range(group):
            r = first + g
            keys[g, 0:capacity, :] = cache_ref[r]
            keys[g, capacity : capacity + steps, :] = fresh_ref[r]
            q = jnp.concatenate([q_ref[r, s] for s in range(steps)], axis=1)
            scores.append(jnp.dot(keys[g], q, preferred_element_type=jnp.float32))
        for g in range(group):
            visible = (position < lens_ref[first_request + i * reqs + first + g]) | fresh_ok
            masked = jnp.where(visible, scores[g] * score_scale, masked_score)
            peak = jnp.max(masked, axis=0, keepdims=True)
            weight = jnp.exp(masked - peak)
            inverse = 1.0 / jnp.sum(weight, axis=0, keepdims=True)
            probs.append((weight * inverse).astype(jnp.bfloat16))
        for g in range(group):
            latent = lax.dot_general(
                probs[g],
                keys[g, :, :LATENT_WIDTH],
                (((0,), (0,)), ((), ())),
                preferred_element_type=jnp.float32,
            )
            rows[g] = latent
        for g in range(group):
            at = (i * reqs + first + g) * steps
            for side in range(2):
                zz = z if side == 0 else 1 - z
                for rel in range(N_X):
                    out = outs[side * N_X + rel]
                    chip = zz * 64 + lax.rem(x + rel, N_X) * 16
                    for s in range(steps):
                        picked = [
                            rows[g, pl.ds(pl.multiple_of(s * heads + chip + core * 8, 8), 8), :]
                            for core in (c, 1 - c)
                        ]
                        out[at + s] = jnp.concatenate(picked, axis=0).astype(jnp.bfloat16)


def attend(lengths, queries, cache, fresh, first, count):
    reqs, steps, width, heads = queries.shape
    capacity = cache.shape[1]
    part = 8
    n = count * steps
    base = first // part
    return pl.pallas_call(
        functools.partial(attend_kernel, first_request=first),
        grid_spec=pltpu.PrefetchScalarGridSpec(
            num_scalar_prefetch=1,
            grid=(count // part,),
            in_specs=[
                pl.BlockSpec((part, steps, width, heads), lambda i, l: (base + i, 0, 0, 0)),
                pl.BlockSpec((part, capacity, width), lambda i, l: (base + i, 0, 0)),
                pl.BlockSpec((part, steps, width), lambda i, l: (base + i, 0, 0)),
            ],
            out_specs=[pl.BlockSpec((n, 16, LATENT_WIDTH), lambda i, l: (0, 0, 0))] * (2 * N_X),
            scratch_shapes=[
                pltpu.VMEM((GROUP, T_PAD, width), jnp.bfloat16),
                pltpu.VMEM((GROUP, steps * heads, LATENT_WIDTH), jnp.float32),
            ],
        ),
        out_shape=[jax.ShapeDtypeStruct((n, 16, LATENT_WIDTH), jnp.bfloat16)] * (2 * N_X),
        compiler_params=pltpu.CompilerParams(vmem_limit_bytes=60 * 1024 * 1024),
        cost_estimate=pl.CostEstimate(
            flops=2 * n * heads * 256 * (width + LATENT_WIDTH),
            bytes_accessed=count * 800_000,
            transcendentals=n * heads * 256,
        ),
        name="attend",
    )(lengths, queries, cache, fresh)


def vmem_out(shape, dtype=jnp.bfloat16):
    return pltpu.VMEM(shape, dtype)


HBM_SPEC = pl.BlockSpec(memory_space=pltpu.HBM)
ANY_SPEC = pl.BlockSpec(memory_space=pl.ANY)
VMEM_SPEC = pl.BlockSpec(memory_space=pltpu.VMEM)


def in_hbm(value):
    return pltpu.with_memory_space_constraint(value, pltpu.HBM)


def run_copies(copies):
    for copy in copies:
        copy.start()
    for copy in copies:
        copy.wait()


def hold_projection_kernel(up_own, up_other, out_own, out_other, up_ref, out_ref, sems):
    half = out_own.shape[0]
    pairs = [
        (up_own, up_ref.at[0:8]),
        (up_other, up_ref.at[8:16]),
        (out_own, out_ref.at[0:half]),
        (out_other, out_ref.at[half : 2 * half]),
    ]
    run_copies([pltpu.make_async_copy(a, b, sems.at[i]) for i, (a, b) in enumerate(pairs)])


def hold_projection(up_own, up_other, out_own, out_other):
    return pl.pallas_call(
        hold_projection_kernel,
        in_specs=[HBM_SPEC, ANY_SPEC] * 2,
        out_specs=[VMEM_SPEC] * 2,
        out_shape=[
            vmem_out((16,) + up_own.shape[1:]),
            vmem_out((2 * out_own.shape[0], out_own.shape[1])),
        ],
        scratch_shapes=[pltpu.SemaphoreType.DMA((4,))],
        cost_estimate=pl.CostEstimate(flops=0, bytes_accessed=17_000_000, transcendentals=0),
        compiler_params=pltpu.CompilerParams(vmem_limit_bytes=16 * 1024 * 1024),
        name="hold_projection",
    )(in_hbm(up_own), up_other, in_hbm(out_own), out_other)


def hold_feed_kernel(g0, g1, u0, u1, d0, d1, own_ref, other_ref, down_ref, sems):
    units = g0.shape[1]
    pairs = []
    for side, (g, u, d) in enumerate(((g0, u0, d0), (g1, u1, d1))):
        mix = (own_ref, other_ref)[side]
        for j in range(units // 128):
            cols = slice(j * 128, (j + 1) * 128)
            pairs.append((g.at[:, cols], mix.at[j, :, 0:128]))
            pairs.append((u.at[:, cols], mix.at[j, :, 128:256]))
        pairs.append((d, down_ref.at[side * units : (side + 1) * units]))
    run_copies([pltpu.make_async_copy(a, b, sems.at[i]) for i, (a, b) in enumerate(pairs)])


def hold_feed(g0, g1, u0, u1, d0, d1):
    width, units = g0.shape
    tiles = units // 128
    return pl.pallas_call(
        hold_feed_kernel,
        in_specs=[HBM_SPEC, ANY_SPEC] * 3,
        out_specs=[VMEM_SPEC] * 3,
        out_shape=[vmem_out((tiles, width, 256))] * 2 + [vmem_out((2 * units, width))],
        scratch_shapes=[pltpu.SemaphoreType.DMA((4 * tiles + 2,))],
        cost_estimate=pl.CostEstimate(flops=0, bytes_accessed=27_500_000, transcendentals=0),
        compiler_params=pltpu.CompilerParams(vmem_limit_bytes=16 * 1024 * 1024),
        name="hold_feed",
    )(in_hbm(g0), g1, in_hbm(u0), u1, in_hbm(d0), d1)


def values_kernel(*refs, blocks):
    lat, up_ref, out_ref, turned = refs[:blocks], refs[blocks], refs[blocks + 1], refs[blocks + 2]
    heads, depth, wide = up_ref.shape
    n = lat[0].shape[0]
    for i, ref in enumerate(lat):

        @pl.loop(0, n)
        def _(r):
            row = ref[r].astype(jnp.float32)
            at = pl.multiple_of(i * n * heads + r * heads, heads)
            for lane in range(depth // 128):
                turned[lane, pl.ds(at, heads), :] = row[:, lane * 128 : (lane + 1) * 128]

    for h in range(heads):
        rows = jnp.concatenate(
            [turned[lane, pl.ds(h, blocks * n, stride=heads), :] for lane in range(depth // 128)],
            axis=1,
        ).astype(jnp.bfloat16)
        part = jnp.dot(rows, up_ref[h], preferred_element_type=jnp.float32)
        out_ref[:, h * wide : (h + 1) * wide] = part.astype(jnp.bfloat16)


def values_of(blocks, up):
    n, heads, depth = blocks[0].shape
    rows = n * len(blocks)
    wide = up.shape[2]
    return pl.pallas_call(
        functools.partial(values_kernel, blocks=len(blocks)),
        in_specs=[VMEM_SPEC] * (len(blocks) + 1),
        out_specs=VMEM_SPEC,
        out_shape=jax.ShapeDtypeStruct((rows, heads * wide), jnp.bfloat16),
        scratch_shapes=[pltpu.VMEM((depth // 128, rows * heads, 128), jnp.float32)],
        compiler_params=pltpu.CompilerParams(vmem_limit_bytes=16 * 1024 * 1024),
        cost_estimate=pl.CostEstimate(
            flops=2 * rows * heads * depth * wide, bytes_accessed=4_000_000, transcendentals=0
        ),
        name="values",
    )(*blocks, up)


def write_rows(part, outs, cols):
    at = 0
    for out in outs:
        size = out.shape[0]
        out[:, cols] = part[at : at + size].astype(out.dtype)
        at += size


def project_kernel(*refs, parts):
    count = len(parts)
    given, w_ref, outs, values = refs[:count], refs[count], refs[count + 1 : -1], refs[-1]
    at = 0
    for ref, (first, size) in zip(given, parts):
        values[at : at + size, :] = ref[first : first + size, :]
        at += size
    tile = 512

    @pl.loop(0, w_ref.shape[1] // tile)
    def _(j):
        cols = pl.ds(pl.multiple_of(j * tile, tile), tile)
        write_rows(
            jnp.dot(values[...], w_ref[:, cols], preferred_element_type=jnp.float32), outs, cols
        )


def project(values, out, shapes):
    parts = [(first, size) for _, first, size in values]
    rows = sum(size for _, size in parts)
    depth, width = out.shape
    return pl.pallas_call(
        functools.partial(project_kernel, parts=parts),
        in_specs=[VMEM_SPEC] * (len(values) + 1),
        out_specs=[VMEM_SPEC] * len(shapes),
        out_shape=[jax.ShapeDtypeStruct((r, width), d) for r, d in shapes],
        scratch_shapes=[pltpu.VMEM((rows, depth), jnp.bfloat16)],
        compiler_params=pltpu.CompilerParams(vmem_limit_bytes=16 * 1024 * 1024),
        cost_estimate=pl.CostEstimate(
            flops=2 * rows * depth * width, bytes_accessed=17_000_000, transcendentals=0
        ),
        name="project",
    )(*[v for v, _, _ in values], out)


def feed_kernel(*refs, blocks):
    given, mixes, down_ref = refs[:blocks], refs[blocks : blocks + 2], refs[blocks + 2]
    *outs, rows, hidden = refs[blocks + 3 :]
    at = 0
    for b in given:
        rows[at : at + b.shape[0], :] = b[...]
        at += b.shape[0]
    tiles = mixes[0].shape[0]
    for side, mix in enumerate(mixes):

        @pl.loop(0, tiles)
        def _(j):
            both = jnp.dot(rows[...], mix[j], preferred_element_type=jnp.float32)
            gate, up_part = both[:, :128], both[:, 128:]
            value = gate / (1.0 + jnp.exp(-gate)) * up_part
            at = pl.multiple_of((side * tiles + j) * 128, 128)
            hidden[:, pl.ds(at, 128)] = value.astype(jnp.bfloat16)

    tile = 512

    @pl.loop(0, down_ref.shape[1] // tile)
    def _(j):
        cols = pl.ds(pl.multiple_of(j * tile, tile), tile)
        write_rows(
            jnp.dot(hidden[...], down_ref[:, cols], preferred_element_type=jnp.float32), outs, cols
        )


def feed(blocks, held, shapes):
    rows = sum(b.shape[0] for b in blocks)
    units, width = held[2].shape
    return pl.pallas_call(
        functools.partial(feed_kernel, blocks=len(blocks)),
        in_specs=[VMEM_SPEC] * (len(blocks) + 3),
        out_specs=[VMEM_SPEC] * len(shapes),
        out_shape=[jax.ShapeDtypeStruct((r, width), d) for r, d in shapes],
        scratch_shapes=[
            pltpu.VMEM((rows, width), jnp.bfloat16),
            pltpu.VMEM((rows, units), jnp.bfloat16),
        ],
        compiler_params=pltpu.CompilerParams(vmem_limit_bytes=16 * 1024 * 1024),
        cost_estimate=pl.CostEstimate(
            flops=6 * rows * width * units, bytes_accessed=28_000_000, transcendentals=rows * units
        ),
        name="feed",
    )(*blocks, *held)


def after(value, *others):
    return lax.optimization_barrier((value,) + others)[0]


SMALL = pltpu.CompilerParams(vmem_limit_bytes=16 * 1024 * 1024)


def glue(kernel, name, args, shapes):
    return pl.pallas_call(
        kernel,
        in_specs=[VMEM_SPEC] * len(args),
        out_specs=[VMEM_SPEC] * len(shapes),
        out_shape=[jax.ShapeDtypeStruct(s, d) for s, d in shapes],
        compiler_params=SMALL,
        cost_estimate=pl.CostEstimate(flops=10_000, bytes_accessed=2_000_000, transcendentals=0),
        name=name,
    )(*args)


def flatten_kernel(hidden_ref, out_ref):
    steps = hidden_ref.shape[1]
    for r in range(hidden_ref.shape[0]):
        out_ref[r * steps : (r + 1) * steps, :] = hidden_ref[r].astype(jnp.float32)


def column_loop(width, body):
    tile = 512

    @pl.loop(0, width // tile)
    def _(j):
        body(pl.ds(pl.multiple_of(j * tile, tile), tile))


def fold_kernel(near_ref, back_ref, out_ref):
    def body(cols):
        total = near_ref[:, cols] + back_ref[:, cols].astype(jnp.float32)
        out_ref[:, cols] = total.astype(jnp.bfloat16)

    column_loop(near_ref.shape[1], body)


def fold(near, back):
    (out,) = glue(fold_kernel, "fold", (near, back), [(near.shape, jnp.bfloat16)])
    return out


def norm_kernel(hidden_ref, gain_ref, own_ref, *refs):
    *received, residual_ref, normed_ref, squares = refs
    width = own_ref.shape[1]
    squares[...] = jnp.zeros_like(squares)

    def add(cols):
        total = hidden_ref[:, cols] + own_ref[:, cols]
        for ref in received:
            total = total + ref[:, cols].astype(jnp.float32)
        residual_ref[:, cols] = total
        square = total * total
        for at in range(0, square.shape[1], 128):
            squares[...] += square[:, at : at + 128]

    column_loop(width, add)
    mean = jnp.sum(squares[...], axis=1, keepdims=True) / width
    scale = lax.rsqrt(mean + norm_eps)

    def write(cols):
        normed_ref[:, cols] = (residual_ref[:, cols] * scale * gain_ref[:, cols]).astype(jnp.bfloat16)

    column_loop(width, write)


def norm(own, received, hidden, gain):
    n, width = own.shape
    return pl.pallas_call(
        norm_kernel,
        in_specs=[VMEM_SPEC] * (3 + len(received)),
        out_specs=[VMEM_SPEC] * 2,
        out_shape=[
            jax.ShapeDtypeStruct((n, width), jnp.float32),
            jax.ShapeDtypeStruct((n, width), jnp.bfloat16),
        ],
        scratch_shapes=[pltpu.VMEM((n, 128), jnp.float32)],
        compiler_params=SMALL,
        cost_estimate=pl.CostEstimate(flops=10_000, bytes_accessed=2_000_000, transcendentals=0),
        name="norm",
    )(hidden, gain, own, *received)


def finish_kernel(residual_ref, own_ref, *refs):
    *received, out_ref = refs

    def body(cols):
        total = residual_ref[:, cols] + own_ref[:, cols]
        for ref in received:
            total = total + ref[:, cols].astype(jnp.float32)
        out_ref[:, cols] = total.astype(jnp.bfloat16)

    column_loop(own_ref.shape[1], body)


def page_kernel(partner_ref, request_ref, count_ref, cache_ref, block_ref, offset_ref):
    dp = lax.axis_index("dp")
    offset_ref[0] = jnp.bitwise_xor(partner_ref[dp], dp)
    for k in range(MIG_MAX):
        rows = cache_ref[0, k * PAGE : (k + 1) * PAGE, :]
        block_ref[k] = jnp.where(k < count_ref[0], rows, jnp.zeros_like(rows))


def page_block(partner, moved_request, moved_pages, cache):
    width = cache.shape[2]
    return pl.pallas_call(
        page_kernel,
        grid_spec=pltpu.PrefetchScalarGridSpec(
            num_scalar_prefetch=3,
            grid=(1,),
            in_specs=[pl.BlockSpec((1,) + cache.shape[1:], lambda i, p, r, c: (r[0], 0, 0))],
            out_specs=[
                pl.BlockSpec((MIG_MAX, PAGE, width), lambda i, p, r, c: (0, 0, 0)),
                pl.BlockSpec(memory_space=pltpu.SMEM),
            ],
        ),
        out_shape=[
            jax.ShapeDtypeStruct((MIG_MAX, PAGE, width), cache.dtype),
            jax.ShapeDtypeStruct((1,), jnp.int32),
        ],
        compiler_params=SMALL,
        cost_estimate=pl.CostEstimate(flops=1_000, bytes_accessed=400_000, transcendentals=0),
        name="pages",
    )(partner.reshape(-1), moved_request, moved_pages, in_hbm(cache))


def pick_kernel(offset_ref, mine_ref, other_ref, out_ref, *, bit):
    trade = lax.rem(offset_ref[0] // (1 << bit), 2) == 1

    @pl.when(trade)
    def _():
        out_ref[...] = other_ref[...]

    @pl.when(jnp.logical_not(trade))
    def _():
        out_ref[...] = mine_ref[...]


def page_trade(block, bit):
    return lax.ppermute(block, "dp", [(d, d ^ (1 << bit)) for d in range(8)])


def page_pick(block, other, offset, bit):
    return pl.pallas_call(
        functools.partial(pick_kernel, bit=bit),
        in_specs=[pl.BlockSpec(memory_space=pltpu.SMEM), VMEM_SPEC, VMEM_SPEC],
        out_specs=VMEM_SPEC,
        out_shape=jax.ShapeDtypeStruct(block.shape, block.dtype),
        compiler_params=SMALL,
        cost_estimate=pl.CostEstimate(flops=1_000, bytes_accessed=400_000, transcendentals=0),
        name="pick",
    )(offset, block, other)


def local(
    request_latent_cache,
    lengths,
    queries,
    incoming_keys,
    hidden_in,
    value_up_weight,
    w_out,
    norm_gain,
    w_gate,
    w_up,
    w_down,
    partner,
    moved_request,
    moved_pages,
):
    req_here, steps_here, width = hidden_in.shape
    n = req_here * steps_here
    up_other, out_other, gate_other = swap_cores(value_up_weight), swap_cores(w_out), swap_cores(w_gate)
    turned = jnp.swapaxes(queries, 2, 3)
    own0, own1, own2, own3, go0, go1, go2, go3 = attend(
        lengths, turned, request_latent_cache, incoming_keys, 0, req_here
    )
    near_shapes = [(n, jnp.float32), (n, jnp.float32), (n, jnp.bfloat16), (n, jnp.float32)]
    far_shapes = [(n, jnp.bfloat16)] * N_X

    go1, go3, own2 = after(go1, up_other), after(go3, up_other), after(own2, up_other)
    far_in1, far_in3 = shift(go1, dz=1), shift(go3, dz=-1)
    near2 = shift(own2, dx=2)
    up2, out2 = hold_projection(value_up_weight, up_other, w_out, out_other)
    block, offset = page_block(
        partner, after(moved_request, out2), moved_pages, request_latent_cache
    )
    traded = page_trade(block, 0)
    first = (near2, far_in1, far_in3, out2, gate_other, traded)
    far1 = shift(after(far_in1, *first), dx=1)
    far3 = shift(after(far_in3, *first), dx=3)
    far_in2, far_in0 = shift(after(go2, *first), dz=-1), shift(after(go0, *first), dz=1)
    far2 = shift(far_in2, dx=2)
    near1 = shift(after(own1, far_in0, far_in2), dx=1)
    near3 = shift(after(own3, far_in0, far_in2), dx=3)
    block = page_pick(block, after(traded, *first), offset, 0)
    block = page_pick(block, after(page_trade(block, 1), far_in0, far_in2), offset, 1)
    second = (far_in0, far_in2, far1, far3, block)
    fup_other = swap_cores(after(w_up, *second))
    down_other = swap_cores(after(w_down, *second))
    (hidden32,) = glue(
        flatten_kernel, "flatten", (after(hidden_in, *first),), [((n, width), jnp.float32)]
    )
    gain = norm_gain.reshape(1, width)
    values_a = values_of([after(own0, far_in0), near2], up2)
    values_b = values_of([far_in0, far1], up2)
    values_c = values_of([far2, far3], up2)
    block = page_pick(block, after(page_trade(block, 2), far2), offset, 2)
    values_b = after(values_b, values_a, block, fup_other, down_other)
    far = project([(values_b, 0, 2 * n), (values_c, 0, 2 * n)], out2, far_shapes)
    back1, back3 = shift(far[1], dz=-1), shift(far[3], dz=1)
    aside = shift(far[2], dx=-2)
    values_d = values_of([after(near1, far[0]), near3], up2)
    near = project(
        [(values_a, 0, n), (values_d, 0, n), (values_a, n, n), (values_d, n, n)], out2, near_shapes
    )
    home2 = shift(near[2], dx=-2)
    back2 = shift(aside, dz=1)
    fold1, fold3 = fold(near[1], back1), fold(near[3], back3)
    home1, home3 = shift(fold1, dx=-1), shift(fold3, dx=-3)
    back0 = shift(after(far[0], fold1, fold3), dz=-1)
    held = hold_feed(after(w_gate, fold1, fold3), gate_other, w_up, fup_other, w_down, down_other)
    residual, normed = norm(
        near[0], [back0, back2, after(home1, held[0]), home2, home3], hidden32, gain
    )

    row1, row3 = shift(normed, dx=1), shift(normed, dx=3)
    over, under = shift(normed, dz=1), shift(normed, dz=-1)
    row2 = shift(normed, dx=2)
    far_row1, far_row3 = shift(row1, dz=1), shift(row3, dz=-1)
    far_row2 = shift(under, dx=2)
    near = feed([normed, row1, row2, row3], held, near_shapes)
    home2 = shift(near[2], dx=-2)
    far = feed([after(over, near[0]), far_row1, far_row2, far_row3], held, far_shapes)
    back1, back3 = shift(far[1], dz=-1), shift(far[3], dz=1)
    aside, back0 = shift(far[2], dx=-2), shift(far[0], dz=-1)
    fold1, fold3 = fold(near[1], back1), fold(near[3], back3)
    home1, home3 = shift(fold1, dx=-1), shift(fold3, dx=-3)
    back2 = shift(aside, dz=1)
    (out,) = glue(
        finish_kernel, "finish", (residual, near[0], back0, back2, home1, home2, home3),
        [((n, width), jnp.bfloat16)],
    )
    return out.reshape(req_here, steps_here, width), block


def solution(mesh):
    in_specs = (
        P(("dp", "tp"), None, None),
        P(("dp", "tp")),
        P(("dp", "tp"), None, None, None),
        P(("dp", "tp"), None, None),
        P(("dp", "tp"), None, None),
        P("tp", None, None),
        P("tp", None),
        P(),
        P(None, "tp"),
        P(None, "tp"),
        P("tp", None),
        P(None, "tp"),
        P(("dp", "tp")),
        P(("dp", "tp")),
    )
    out_specs = (P(("dp", "tp"), None, None), P(("dp", "tp"), None, None))
    return jax.shard_map(local, mesh=mesh, in_specs=in_specs, out_specs=out_specs, check_vma=False)
```

```python
import functools

import jax
import jax.numpy as jnp
from jax import lax
from jax.experimental import pallas as pl
from jax.experimental.pallas import tpu as pltpu
from jax.sharding import PartitionSpec as P

LATENT_WIDTH = 512
PAGE = 64
MIG_MAX = 2
N_X = 4
N_Z = 4
N_Y = 4
GRID = ("dp", "tp")
T_PAD = 208
GROUP = 8

score_scale = 192.0 ** (-0.5)
masked_score = -1e30
norm_eps = 1e-06


def place(index):
    d, t = index // 16, index % 16
    return (d // 4) * 2 + t // 8, d % 4, (t // 2) % 4, t % 2


def index_of(z, y, x, c):
    z, y, x = z % N_Z, y % N_Y, x % N_X
    return ((z // 2) * 4 + y) * 16 + (z % 2) * 8 + x * 2 + c


def shift(value, dx=0, dz=0):
    pairs = []
    for i in range(128):
        z, y, x, c = place(i)
        pairs.append((i, index_of(z + dz, y, x + dx, c)))
    return lax.ppermute(value, GRID, pairs)


def swap_cores(value):
    return lax.ppermute(value, "tp", [(t, t ^ 1) for t in range(16)])


def attend_kernel(lens_ref, q_ref, cache_ref, fresh_ref, *rest, first_request):
    *outs, keys, rows = rest
    i = pl.program_id(0)
    reqs, steps, width, heads = q_ref.shape
    capacity = cache_ref.shape[1]
    total = keys.shape[1]

    @pl.when(i == 0)
    def _():
        keys[...] = jnp.zeros_like(keys)

    position = lax.broadcasted_iota(jnp.int32, (total, steps * heads), 0)
    column = lax.broadcasted_iota(jnp.int32, (total, steps * heads), 1)
    fresh_ok = (position >= capacity) & (position - capacity <= column // heads)
    t = lax.axis_index("tp")
    z, x, c = t // 8, lax.rem(t // 2, N_X), lax.rem(t, 2)
    group = keys.shape[0]
    for first in range(0, reqs, group):
        scores, probs = [], []
        for g in range(group):
            r = first + g
            keys[g, 0:capacity, :] = cache_ref[r]
            keys[g, capacity : capacity + steps, :] = fresh_ref[r]
            q = jnp.concatenate([q_ref[r, s] for s in range(steps)], axis=1)
            scores.append(jnp.dot(keys[g], q, preferred_element_type=jnp.float32))
        for g in range(group):
            visible = (position < lens_ref[first_request + i * reqs + first + g]) | fresh_ok
            masked = jnp.where(visible, scores[g] * score_scale, masked_score)
            peak = jnp.max(masked, axis=0, keepdims=True)
            weight = jnp.exp(masked - peak)
            inverse = 1.0 / jnp.sum(weight, axis=0, keepdims=True)
            probs.append((weight * inverse).astype(jnp.bfloat16))
        for g in range(group):
            latent = lax.dot_general(
                probs[g],
                keys[g, :, :LATENT_WIDTH],
                (((0,), (0,)), ((), ())),
                preferred_element_type=jnp.float32,
            )
            rows[g] = latent
        for g in range(group):
            at = (i * reqs + first + g) * steps
            for side in range(2):
                zz = z if side == 0 else 1 - z
                for rel in range(N_X):
                    out = outs[side * N_X + rel]
                    chip = zz * 64 + lax.rem(x + rel, N_X) * 16
                    for s in range(steps):
                        picked = [
                            rows[g, pl.ds(pl.multiple_of(s * heads + chip + core * 8, 8), 8), :]
                            for core in (c, 1 - c)
                        ]
                        out[at + s] = jnp.concatenate(picked, axis=0).astype(jnp.bfloat16)


def attend(lengths, queries, cache, fresh, first, count):
    reqs, steps, width, heads = queries.shape
    capacity = cache.shape[1]
    part = 8
    n = count * steps
    base = first // part
    return pl.pallas_call(
        functools.partial(attend_kernel, first_request=first),
        grid_spec=pltpu.PrefetchScalarGridSpec(
            num_scalar_prefetch=1,
            grid=(count // part,),
            in_specs=[
                pl.BlockSpec((part, steps, width, heads), lambda i, l: (base + i, 0, 0, 0)),
                pl.BlockSpec((part, capacity, width), lambda i, l: (base + i, 0, 0)),
                pl.BlockSpec((part, steps, width), lambda i, l: (base + i, 0, 0)),
            ],
            out_specs=[pl.BlockSpec((n, 16, LATENT_WIDTH), lambda i, l: (0, 0, 0))] * (2 * N_X),
            scratch_shapes=[
                pltpu.VMEM((GROUP, T_PAD, width), jnp.bfloat16),
                pltpu.VMEM((GROUP, steps * heads, LATENT_WIDTH), jnp.float32),
            ],
        ),
        out_shape=[jax.ShapeDtypeStruct((n, 16, LATENT_WIDTH), jnp.bfloat16)] * (2 * N_X),
        compiler_params=pltpu.CompilerParams(vmem_limit_bytes=60 * 1024 * 1024),
        cost_estimate=pl.CostEstimate(
            flops=2 * n * heads * 256 * (width + LATENT_WIDTH),
            bytes_accessed=count * 800_000,
            transcendentals=n * heads * 256,
        ),
        name="attend",
    )(lengths, queries, cache, fresh)


def vmem_out(shape, dtype=jnp.bfloat16):
    return pltpu.VMEM(shape, dtype)


HBM_SPEC = pl.BlockSpec(memory_space=pltpu.HBM)
ANY_SPEC = pl.BlockSpec(memory_space=pl.ANY)
VMEM_SPEC = pl.BlockSpec(memory_space=pltpu.VMEM)


def in_hbm(value):
    return pltpu.with_memory_space_constraint(value, pltpu.HBM)


def run_copies(copies):
    for copy in copies:
        copy.start()
    for copy in copies:
        copy.wait()


def hold_projection_kernel(up_own, up_other, out_own, out_other, up_ref, out_ref, sems):
    half = out_own.shape[0]
    pairs = [
        (up_own, up_ref.at[0:8]),
        (up_other, up_ref.at[8:16]),
        (out_own, out_ref.at[0:half]),
        (out_other, out_ref.at[half : 2 * half]),
    ]
    run_copies([pltpu.make_async_copy(a, b, sems.at[i]) for i, (a, b) in enumerate(pairs)])


def hold_projection(up_own, up_other, out_own, out_other):
    return pl.pallas_call(
        hold_projection_kernel,
        in_specs=[HBM_SPEC, ANY_SPEC] * 2,
        out_specs=[VMEM_SPEC] * 2,
        out_shape=[
            vmem_out((16,) + up_own.shape[1:]),
            vmem_out((2 * out_own.shape[0], out_own.shape[1])),
        ],
        scratch_shapes=[pltpu.SemaphoreType.DMA((4,))],
        cost_estimate=pl.CostEstimate(flops=0, bytes_accessed=17_000_000, transcendentals=0),
        compiler_params=pltpu.CompilerParams(vmem_limit_bytes=16 * 1024 * 1024),
        name="hold_projection",
    )(in_hbm(up_own), up_other, in_hbm(out_own), out_other)


def hold_feed_kernel(g0, g1, u0, u1, d0, d1, own_ref, other_ref, down_ref, sems):
    units = g0.shape[1]
    pairs = []
    for side, (g, u, d) in enumerate(((g0, u0, d0), (g1, u1, d1))):
        mix = (own_ref, other_ref)[side]
        for j in range(units // 128):
            cols = slice(j * 128, (j + 1) * 128)
            pairs.append((g.at[:, cols], mix.at[j, :, 0:128]))
            pairs.append((u.at[:, cols], mix.at[j, :, 128:256]))
        pairs.append((d, down_ref.at[side * units : (side + 1) * units]))
    run_copies([pltpu.make_async_copy(a, b, sems.at[i]) for i, (a, b) in enumerate(pairs)])


def hold_feed(g0, g1, u0, u1, d0, d1):
    width, units = g0.shape
    tiles = units // 128
    return pl.pallas_call(
        hold_feed_kernel,
        in_specs=[HBM_SPEC, ANY_SPEC] * 3,
        out_specs=[VMEM_SPEC] * 3,
        out_shape=[vmem_out((tiles, width, 256))] * 2 + [vmem_out((2 * units, width))],
        scratch_shapes=[pltpu.SemaphoreType.DMA((4 * tiles + 2,))],
        cost_estimate=pl.CostEstimate(flops=0, bytes_accessed=27_500_000, transcendentals=0),
        compiler_params=pltpu.CompilerParams(vmem_limit_bytes=16 * 1024 * 1024),
        name="hold_feed",
    )(in_hbm(g0), g1, in_hbm(u0), u1, in_hbm(d0), d1)


def values_kernel(*refs, blocks):
    lat, up_ref, out_ref, turned = refs[:blocks], refs[blocks], refs[blocks + 1], refs[blocks + 2]
    heads, depth, wide = up_ref.shape
    n = lat[0].shape[0]
    for i, ref in enumerate(lat):

        @pl.loop(0, n)
        def _(r):
            row = ref[r].astype(jnp.float32)
            at = pl.multiple_of(i * n * heads + r * heads, heads)
            for lane in range(depth // 128):
                turned[lane, pl.ds(at, heads), :] = row[:, lane * 128 : (lane + 1) * 128]

    for h in range(heads):
        rows = jnp.concatenate(
            [turned[lane, pl.ds(h, blocks * n, stride=heads), :] for lane in range(depth // 128)],
            axis=1,
        ).astype(jnp.bfloat16)
        part = jnp.dot(rows, up_ref[h], preferred_element_type=jnp.float32)
        out_ref[:, h * wide : (h + 1) * wide] = part.astype(jnp.bfloat16)


def values_of(blocks, up):
    n, heads, depth = blocks[0].shape
    rows = n * len(blocks)
    wide = up.shape[2]
    return pl.pallas_call(
        functools.partial(values_kernel, blocks=len(blocks)),
        in_specs=[VMEM_SPEC] * (len(blocks) + 1),
        out_specs=VMEM_SPEC,
        out_shape=jax.ShapeDtypeStruct((rows, heads * wide), jnp.bfloat16),
        scratch_shapes=[pltpu.VMEM((depth // 128, rows * heads, 128), jnp.float32)],
        compiler_params=pltpu.CompilerParams(vmem_limit_bytes=16 * 1024 * 1024),
        cost_estimate=pl.CostEstimate(
            flops=2 * rows * heads * depth * wide, bytes_accessed=4_000_000, transcendentals=0
        ),
        name="values",
    )(*blocks, up)


def write_rows(part, outs, cols):
    at = 0
    for out in outs:
        size = out.shape[0]
        out[:, cols] = part[at : at + size].astype(out.dtype)
        at += size


def project_kernel(*refs, parts):
    count = len(parts)
    given, w_ref, outs, values = refs[:count], refs[count], refs[count + 1 : -1], refs[-1]
    at = 0
    for ref, (first, size) in zip(given, parts):
        values[at : at + size, :] = ref[first : first + size, :]
        at += size
    tile = 512

    @pl.loop(0, w_ref.shape[1] // tile)
    def _(j):
        cols = pl.ds(pl.multiple_of(j * tile, tile), tile)
        write_rows(
            jnp.dot(values[...], w_ref[:, cols], preferred_element_type=jnp.float32), outs, cols
        )


def project(values, out, shapes):
    parts = [(first, size) for _, first, size in values]
    rows = sum(size for _, size in parts)
    depth, width = out.shape
    return pl.pallas_call(
        functools.partial(project_kernel, parts=parts),
        in_specs=[VMEM_SPEC] * (len(values) + 1),
        out_specs=[VMEM_SPEC] * len(shapes),
        out_shape=[jax.ShapeDtypeStruct((r, width), d) for r, d in shapes],
        scratch_shapes=[pltpu.VMEM((rows, depth), jnp.bfloat16)],
        compiler_params=pltpu.CompilerParams(vmem_limit_bytes=16 * 1024 * 1024),
        cost_estimate=pl.CostEstimate(
            flops=2 * rows * depth * width, bytes_accessed=17_000_000, transcendentals=0
        ),
        name="project",
    )(*[v for v, _, _ in values], out)


def feed_kernel(*refs, blocks):
    given, mixes, down_ref = refs[:blocks], refs[blocks : blocks + 2], refs[blocks + 2]
    *outs, rows, hidden = refs[blocks + 3 :]
    at = 0
    for b in given:
        rows[at : at + b.shape[0], :] = b[...]
        at += b.shape[0]
    tiles = mixes[0].shape[0]
    for side, mix in enumerate(mixes):

        @pl.loop(0, tiles)
        def _(j):
            both = jnp.dot(rows[...], mix[j], preferred_element_type=jnp.float32)
            gate, up_part = both[:, :128], both[:, 128:]
            value = gate / (1.0 + jnp.exp(-gate)) * up_part
            at = pl.multiple_of((side * tiles + j) * 128, 128)
            hidden[:, pl.ds(at, 128)] = value.astype(jnp.bfloat16)

    tile = 512

    @pl.loop(0, down_ref.shape[1] // tile)
    def _(j):
        cols = pl.ds(pl.multiple_of(j * tile, tile), tile)
        write_rows(
            jnp.dot(hidden[...], down_ref[:, cols], preferred_element_type=jnp.float32), outs, cols
        )


def feed(blocks, held, shapes):
    rows = sum(b.shape[0] for b in blocks)
    units, width = held[2].shape
    return pl.pallas_call(
        functools.partial(feed_kernel, blocks=len(blocks)),
        in_specs=[VMEM_SPEC] * (len(blocks) + 3),
        out_specs=[VMEM_SPEC] * len(shapes),
        out_shape=[jax.ShapeDtypeStruct((r, width), d) for r, d in shapes],
        scratch_shapes=[
            pltpu.VMEM((rows, width), jnp.bfloat16),
            pltpu.VMEM((rows, units), jnp.bfloat16),
        ],
        compiler_params=pltpu.CompilerParams(vmem_limit_bytes=16 * 1024 * 1024),
        cost_estimate=pl.CostEstimate(
            flops=6 * rows * width * units, bytes_accessed=28_000_000, transcendentals=rows * units
        ),
        name="feed",
    )(*blocks, *held)


def after(value, *others):
    return lax.optimization_barrier((value,) + others)[0]


SMALL = pltpu.CompilerParams(vmem_limit_bytes=16 * 1024 * 1024)


def glue(kernel, name, args, shapes):
    return pl.pallas_call(
        kernel,
        in_specs=[VMEM_SPEC] * len(args),
        out_specs=[VMEM_SPEC] * len(shapes),
        out_shape=[jax.ShapeDtypeStruct(s, d) for s, d in shapes],
        compiler_params=SMALL,
        cost_estimate=pl.CostEstimate(flops=10_000, bytes_accessed=2_000_000, transcendentals=0),
        name=name,
    )(*args)


def flatten_kernel(hidden_ref, out_ref):
    steps = hidden_ref.shape[1]
    for r in range(hidden_ref.shape[0]):
        out_ref[r * steps : (r + 1) * steps, :] = hidden_ref[r].astype(jnp.float32)


def column_loop(width, body):
    tile = 512

    @pl.loop(0, width // tile)
    def _(j):
        body(pl.ds(pl.multiple_of(j * tile, tile), tile))


def fold_kernel(near_ref, back_ref, out_ref):
    def body(cols):
        total = near_ref[:, cols] + back_ref[:, cols].astype(jnp.float32)
        out_ref[:, cols] = total.astype(jnp.bfloat16)

    column_loop(near_ref.shape[1], body)


def fold(near, back):
    (out,) = glue(fold_kernel, "fold", (near, back), [(near.shape, jnp.bfloat16)])
    return out


def norm_kernel(hidden_ref, gain_ref, own_ref, *refs):
    *received, residual_ref, normed_ref, squares = refs
    width = own_ref.shape[1]
    squares[...] = jnp.zeros_like(squares)

    def add(cols):
        total = hidden_ref[:, cols] + own_ref[:, cols]
        for ref in received:
            total = total + ref[:, cols].astype(jnp.float32)
        residual_ref[:, cols] = total
        square = total * total
        for at in range(0, square.shape[1], 128):
            squares[...] += square[:, at : at + 128]

    column_loop(width, add)
    mean = jnp.sum(squares[...], axis=1, keepdims=True) / width
    scale = lax.rsqrt(mean + norm_eps)

    def write(cols):
        normed_ref[:, cols] = (residual_ref[:, cols] * scale * gain_ref[:, cols]).astype(jnp.bfloat16)

    column_loop(width, write)


def norm(own, received, hidden, gain):
    n, width = own.shape
    return pl.pallas_call(
        norm_kernel,
        in_specs=[VMEM_SPEC] * (3 + len(received)),
        out_specs=[VMEM_SPEC] * 2,
        out_shape=[
            jax.ShapeDtypeStruct((n, width), jnp.float32),
            jax.ShapeDtypeStruct((n, width), jnp.bfloat16),
        ],
        scratch_shapes=[pltpu.VMEM((n, 128), jnp.float32)],
        compiler_params=SMALL,
        cost_estimate=pl.CostEstimate(flops=10_000, bytes_accessed=2_000_000, transcendentals=0),
        name="norm",
    )(hidden, gain, own, *received)


def finish_kernel(residual_ref, own_ref, *refs):
    *received, out_ref = refs

    def body(cols):
        total = residual_ref[:, cols] + own_ref[:, cols]
        for ref in received:
            total = total + ref[:, cols].astype(jnp.float32)
        out_ref[:, cols] = total.astype(jnp.bfloat16)

    column_loop(own_ref.shape[1], body)


def page_kernel(partner_ref, request_ref, count_ref, cache_ref, block_ref, offset_ref):
    dp = lax.axis_index("dp")
    offset_ref[0] = jnp.bitwise_xor(partner_ref[dp], dp)
    for k in range(MIG_MAX):
        rows = cache_ref[0, k * PAGE : (k + 1) * PAGE, :]
        block_ref[k] = jnp.where(k < count_ref[0], rows, jnp.zeros_like(rows))


def page_block(partner, moved_request, moved_pages, cache):
    width = cache.shape[2]
    return pl.pallas_call(
        page_kernel,
        grid_spec=pltpu.PrefetchScalarGridSpec(
            num_scalar_prefetch=3,
            grid=(1,),
            in_specs=[pl.BlockSpec((1,) + cache.shape[1:], lambda i, p, r, c: (r[0], 0, 0))],
            out_specs=[
                pl.BlockSpec((MIG_MAX, PAGE, width), lambda i, p, r, c: (0, 0, 0)),
                pl.BlockSpec(memory_space=pltpu.SMEM),
            ],
        ),
        out_shape=[
            jax.ShapeDtypeStruct((MIG_MAX, PAGE, width), cache.dtype),
            jax.ShapeDtypeStruct((1,), jnp.int32),
        ],
        compiler_params=SMALL,
        cost_estimate=pl.CostEstimate(flops=1_000, bytes_accessed=400_000, transcendentals=0),
        name="pages",
    )(partner.reshape(-1), moved_request, moved_pages, in_hbm(cache))


def pick_kernel(offset_ref, mine_ref, other_ref, out_ref, *, bit):
    trade = lax.rem(offset_ref[0] // (1 << bit), 2) == 1

    @pl.when(trade)
    def _():
        out_ref[...] = other_ref[...]

    @pl.when(jnp.logical_not(trade))
    def _():
        out_ref[...] = mine_ref[...]


def page_trade(block, bit):
    return lax.ppermute(block, "dp", [(d, d ^ (1 << bit)) for d in range(8)])


def page_pick(block, other, offset, bit):
    return pl.pallas_call(
        functools.partial(pick_kernel, bit=bit),
        in_specs=[pl.BlockSpec(memory_space=pltpu.SMEM), VMEM_SPEC, VMEM_SPEC],
        out_specs=VMEM_SPEC,
        out_shape=jax.ShapeDtypeStruct(block.shape, block.dtype),
        compiler_params=SMALL,
        cost_estimate=pl.CostEstimate(flops=1_000, bytes_accessed=400_000, transcendentals=0),
        name="pick",
    )(offset, block, other)


def local(
    request_latent_cache,
    lengths,
    queries,
    incoming_keys,
    hidden_in,
    value_up_weight,
    w_out,
    norm_gain,
    w_gate,
    w_up,
    w_down,
    partner,
    moved_request,
    moved_pages,
):
    req_here, steps_here, width = hidden_in.shape
    n = req_here * steps_here
    up_other, out_other, gate_other = swap_cores(value_up_weight), swap_cores(w_out), swap_cores(w_gate)
    turned = jnp.swapaxes(queries, 2, 3)
    own0, own1, own2, own3, go0, go1, go2, go3 = attend(
        lengths, turned, request_latent_cache, incoming_keys, 0, req_here
    )
    near_shapes = [(n, jnp.float32), (n, jnp.float32), (n, jnp.bfloat16), (n, jnp.float32)]
    far_shapes = [(n, jnp.bfloat16)] * N_X

    go1, go3, own2 = after(go1, up_other), after(go3, up_other), after(own2, up_other)
    far_in1, far_in3 = shift(go1, dz=1), shift(go3, dz=-1)
    near2 = shift(own2, dx=2)
    up2, out2 = hold_projection(value_up_weight, up_other, w_out, out_other)
    block, offset = page_block(
        partner, after(moved_request, out2), moved_pages, request_latent_cache
    )
    traded = page_trade(block, 0)
    first = (near2, far_in1, far_in3, out2, gate_other, traded)
    far1 = shift(after(far_in1, *first), dx=1)
    far3 = shift(after(far_in3, *first), dx=3)
    far_in2, far_in0 = shift(after(go2, *first), dz=-1), shift(after(go0, *first), dz=1)
    far2 = shift(far_in2, dx=2)
    near1 = shift(after(own1, far_in0, far_in2), dx=1)
    near3 = shift(after(own3, far_in0, far_in2), dx=3)
    block = page_pick(block, after(traded, *first), offset, 0)
    block = page_pick(block, after(page_trade(block, 1), far_in0, far_in2), offset, 1)
    second = (far_in0, far_in2, far1, far3, block)
    fup_other = swap_cores(after(w_up, *second))
    down_other = swap_cores(after(w_down, *second))
    (hidden32,) = glue(
        flatten_kernel, "flatten", (after(hidden_in, *first),), [((n, width), jnp.float32)]
    )
    gain = norm_gain.reshape(1, width)
    values_a = values_of([after(own0, far_in0), near2], up2)
    values_b = values_of([far_in0, far1], up2)
    values_c = values_of([far2, far3], up2)
    block = page_pick(block, after(page_trade(block, 2), far2), offset, 2)
    values_b = after(values_b, values_a, block, fup_other, down_other)
    far = project([(values_b, 0, 2 * n), (values_c, 0, 2 * n)], out2, far_shapes)
    back1, back3 = shift(far[1], dz=-1), shift(far[3], dz=1)
    aside = shift(far[2], dx=-2)
    values_d = values_of([after(near1, far[0]), near3], up2)
    near = project(
        [(values_a, 0, n), (values_d, 0, n), (values_a, n, n), (values_d, n, n)], out2, near_shapes
    )
    home2 = shift(near[2], dx=-2)
    back2 = shift(aside, dz=1)
    fold1, fold3 = fold(near[1], back1), fold(near[3], back3)
    home1, home3 = shift(fold1, dx=-1), shift(fold3, dx=-3)
    back0 = shift(after(far[0], fold1, fold3), dz=-1)
    held = hold_feed(after(w_gate, fold1, fold3), gate_other, w_up, fup_other, w_down, down_other)
    residual, normed = norm(
        near[0], [back0, back2, after(home1, held[0]), home2, home3], hidden32, gain
    )

    row1, row3 = shift(normed, dx=1), shift(normed, dx=3)
    over, under = shift(normed, dz=1), shift(normed, dz=-1)
    row2 = shift(normed, dx=2)
    far_row1, far_row3 = shift(row1, dz=1), shift(row3, dz=-1)
    far_row2 = shift(after(under, row3), dx=2)
    near = feed([normed, row1, row2, row3], held, near_shapes)
    home2 = shift(near[2], dx=-2)
    far = feed([after(over, near[0]), far_row1, far_row2, far_row3], held, far_shapes)
    back1, back3 = shift(far[1], dz=-1), shift(far[3], dz=1)
    aside, back0 = shift(far[2], dx=-2), shift(far[0], dz=-1)
    fold1, fold3 = fold(near[1], back1), fold(near[3], back3)
    home1, home3 = shift(fold1, dx=-1), shift(fold3, dx=-3)
    back2 = shift(aside, dz=1)
    (out,) = glue(
        finish_kernel, "finish", (residual, near[0], back0, back2, home1, home2, home3),
        [((n, width), jnp.bfloat16)],
    )
    return out.reshape(req_here, steps_here, width), block


def solution(mesh):
    in_specs = (
        P(("dp", "tp"), None, None),
        P(("dp", "tp")),
        P(("dp", "tp"), None, None, None),
        P(("dp", "tp"), None, None),
        P(("dp", "tp"), None, None),
        P("tp", None, None),
        P("tp", None),
        P(),
        P(None, "tp"),
        P(None, "tp"),
        P("tp", None),
        P(None, "tp"),
        P(("dp", "tp")),
        P(("dp", "tp")),
    )
    out_specs = (P(("dp", "tp"), None, None), P(("dp", "tp"), None, None))
    return jax.shard_map(local, mesh=mesh, in_specs=in_specs, out_specs=out_specs, check_vma=False)
```

```python
import functools

import jax
import jax.numpy as jnp
from jax import lax
from jax.experimental import pallas as pl
from jax.experimental.pallas import tpu as pltpu
from jax.sharding import PartitionSpec as P

LATENT_WIDTH = 512
PAGE = 64
MIG_MAX = 2
N_X = 4
N_Z = 4
N_Y = 4
GRID = ("dp", "tp")
T_PAD = 208
GROUP = 8

score_scale = 192.0 ** (-0.5)
masked_score = -1e30
norm_eps = 1e-06


def place(index):
    d, t = index // 16, index % 16
    return (d // 4) * 2 + t // 8, d % 4, (t // 2) % 4, t % 2


def index_of(z, y, x, c):
    z, y, x = z % N_Z, y % N_Y, x % N_X
    return ((z // 2) * 4 + y) * 16 + (z % 2) * 8 + x * 2 + c


def shift(value, dx=0, dz=0):
    pairs = []
    for i in range(128):
        z, y, x, c = place(i)
        pairs.append((i, index_of(z + dz, y, x + dx, c)))
    return lax.ppermute(value, GRID, pairs)


def swap_cores(value):
    return lax.ppermute(value, "tp", [(t, t ^ 1) for t in range(16)])


def attend_kernel(lens_ref, q_ref, cache_ref, fresh_ref, *rest, first_request):
    *outs, keys, rows = rest
    i = pl.program_id(0)
    reqs, steps, width, heads = q_ref.shape
    capacity = cache_ref.shape[1]
    total = keys.shape[1]

    @pl.when(i == 0)
    def _():
        keys[...] = jnp.zeros_like(keys)

    position = lax.broadcasted_iota(jnp.int32, (total, steps * heads), 0)
    column = lax.broadcasted_iota(jnp.int32, (total, steps * heads), 1)
    fresh_ok = (position >= capacity) & (position - capacity <= column // heads)
    t = lax.axis_index("tp")
    z, x, c = t // 8, lax.rem(t // 2, N_X), lax.rem(t, 2)
    group = keys.shape[0]
    for first in range(0, reqs, group):
        scores, probs = [], []
        for g in range(group):
            r = first + g
            keys[g, 0:capacity, :] = cache_ref[r]
            keys[g, capacity : capacity + steps, :] = fresh_ref[r]
            q = jnp.concatenate([q_ref[r, s] for s in range(steps)], axis=1)
            scores.append(jnp.dot(keys[g], q, preferred_element_type=jnp.float32))
        for g in range(group):
            visible = (position < lens_ref[first_request + i * reqs + first + g]) | fresh_ok
            masked = jnp.where(visible, scores[g] * score_scale, masked_score)
            peak = jnp.max(masked, axis=0, keepdims=True)
            weight = jnp.exp(masked - peak)
            inverse = 1.0 / jnp.sum(weight, axis=0, keepdims=True)
            probs.append((weight * inverse).astype(jnp.bfloat16))
        for g in range(group):
            latent = lax.dot_general(
                probs[g],
                keys[g, :, :LATENT_WIDTH],
                (((0,), (0,)), ((), ())),
                preferred_element_type=jnp.float32,
            )
            rows[g] = latent
        for g in range(group):
            at = (i * reqs + first + g) * steps
            for side in range(2):
                zz = z if side == 0 else 1 - z
                for rel in range(N_X):
                    out = outs[side * N_X + rel]
                    chip = zz * 64 + lax.rem(x + rel, N_X) * 16
                    for s in range(steps):
                        picked = [
                            rows[g, pl.ds(pl.multiple_of(s * heads + chip + core * 8, 8), 8), :]
                            for core in (c, 1 - c)
                        ]
                        out[at + s] = jnp.concatenate(picked, axis=0).astype(jnp.bfloat16)


def attend(lengths, queries, cache, fresh, first, count):
    reqs, steps, width, heads = queries.shape
    capacity = cache.shape[1]
    part = 8
    n = count * steps
    base = first // part
    return pl.pallas_call(
        functools.partial(attend_kernel, first_request=first),
        grid_spec=pltpu.PrefetchScalarGridSpec(
            num_scalar_prefetch=1,
            grid=(count // part,),
            in_specs=[
                pl.BlockSpec((part, steps, width, heads), lambda i, l: (base + i, 0, 0, 0)),
                pl.BlockSpec((part, capacity, width), lambda i, l: (base + i, 0, 0)),
                pl.BlockSpec((part, steps, width), lambda i, l: (base + i, 0, 0)),
            ],
            out_specs=[pl.BlockSpec((n, 16, LATENT_WIDTH), lambda i, l: (0, 0, 0))] * (2 * N_X),
            scratch_shapes=[
                pltpu.VMEM((GROUP, T_PAD, width), jnp.bfloat16),
                pltpu.VMEM((GROUP, steps * heads, LATENT_WIDTH), jnp.float32),
            ],
        ),
        out_shape=[jax.ShapeDtypeStruct((n, 16, LATENT_WIDTH), jnp.bfloat16)] * (2 * N_X),
        compiler_params=pltpu.CompilerParams(vmem_limit_bytes=60 * 1024 * 1024),
        cost_estimate=pl.CostEstimate(
            flops=2 * n * heads * 256 * (width + LATENT_WIDTH),
            bytes_accessed=count * 800_000,
            transcendentals=n * heads * 256,
        ),
        name="attend",
    )(lengths, queries, cache, fresh)


def vmem_out(shape, dtype=jnp.bfloat16):
    return pltpu.VMEM(shape, dtype)


HBM_SPEC = pl.BlockSpec(memory_space=pltpu.HBM)
ANY_SPEC = pl.BlockSpec(memory_space=pl.ANY)
VMEM_SPEC = pl.BlockSpec(memory_space=pltpu.VMEM)


def in_hbm(value):
    return pltpu.with_memory_space_constraint(value, pltpu.HBM)


def run_copies(copies):
    for copy in copies:
        copy.start()
    for copy in copies:
        copy.wait()


def hold_projection_kernel(up_own, up_other, out_own, out_other, up_ref, out_ref, sems):
    half = out_own.shape[0]
    pairs = [
        (up_own, up_ref.at[0:8]),
        (up_other, up_ref.at[8:16]),
        (out_own, out_ref.at[0:half]),
        (out_other, out_ref.at[half : 2 * half]),
    ]
    run_copies([pltpu.make_async_copy(a, b, sems.at[i]) for i, (a, b) in enumerate(pairs)])


def hold_projection(up_own, up_other, out_own, out_other):
    return pl.pallas_call(
        hold_projection_kernel,
        in_specs=[HBM_SPEC, ANY_SPEC] * 2,
        out_specs=[VMEM_SPEC] * 2,
        out_shape=[
            vmem_out((16,) + up_own.shape[1:]),
            vmem_out((2 * out_own.shape[0], out_own.shape[1])),
        ],
        scratch_shapes=[pltpu.SemaphoreType.DMA((4,))],
        cost_estimate=pl.CostEstimate(flops=0, bytes_accessed=17_000_000, transcendentals=0),
        compiler_params=pltpu.CompilerParams(vmem_limit_bytes=16 * 1024 * 1024),
        name="hold_projection",
    )(in_hbm(up_own), up_other, in_hbm(out_own), out_other)


def hold_feed_kernel(g0, g1, u0, u1, d0, d1, own_ref, other_ref, down_ref, sems):
    units = g0.shape[1]
    pairs = []
    for side, (g, u, d) in enumerate(((g0, u0, d0), (g1, u1, d1))):
        mix = (own_ref, other_ref)[side]
        for j in range(units // 128):
            cols = slice(j * 128, (j + 1) * 128)
            pairs.append((g.at[:, cols], mix.at[j, :, 0:128]))
            pairs.append((u.at[:, cols], mix.at[j, :, 128:256]))
        pairs.append((d, down_ref.at[side * units : (side + 1) * units]))
    run_copies([pltpu.make_async_copy(a, b, sems.at[i]) for i, (a, b) in enumerate(pairs)])


def hold_feed(g0, g1, u0, u1, d0, d1):
    width, units = g0.shape
    tiles = units // 128
    return pl.pallas_call(
        hold_feed_kernel,
        in_specs=[HBM_SPEC, ANY_SPEC] * 3,
        out_specs=[VMEM_SPEC] * 3,
        out_shape=[vmem_out((tiles, width, 256))] * 2 + [vmem_out((2 * units, width))],
        scratch_shapes=[pltpu.SemaphoreType.DMA((4 * tiles + 2,))],
        cost_estimate=pl.CostEstimate(flops=0, bytes_accessed=27_500_000, transcendentals=0),
        compiler_params=pltpu.CompilerParams(vmem_limit_bytes=16 * 1024 * 1024),
        name="hold_feed",
    )(in_hbm(g0), g1, in_hbm(u0), u1, in_hbm(d0), d1)


def values_kernel(*refs, blocks):
    lat, up_ref, out_ref, turned = refs[:blocks], refs[blocks], refs[blocks + 1], refs[blocks + 2]
    heads, depth, wide = up_ref.shape
    n = lat[0].shape[0]
    for i, ref in enumerate(lat):

        @pl.loop(0, n)
        def _(r):
            row = ref[r].astype(jnp.float32)
            at = pl.multiple_of(i * n * heads + r * heads, heads)
            for lane in range(depth // 128):
                turned[lane, pl.ds(at, heads), :] = row[:, lane * 128 : (lane + 1) * 128]

    for h in range(heads):
        rows = jnp.concatenate(
            [turned[lane, pl.ds(h, blocks * n, stride=heads), :] for lane in range(depth // 128)],
            axis=1,
        ).astype(jnp.bfloat16)
        part = jnp.dot(rows, up_ref[h], preferred_element_type=jnp.float32)
        out_ref[:, h * wide : (h + 1) * wide] = part.astype(jnp.bfloat16)


def values_of(blocks, up):
    n, heads, depth = blocks[0].shape
    rows = n * len(blocks)
    wide = up.shape[2]
    return pl.pallas_call(
        functools.partial(values_kernel, blocks=len(blocks)),
        in_specs=[VMEM_SPEC] * (len(blocks) + 1),
        out_specs=VMEM_SPEC,
        out_shape=jax.ShapeDtypeStruct((rows, heads * wide), jnp.bfloat16),
        scratch_shapes=[pltpu.VMEM((depth // 128, rows * heads, 128), jnp.float32)],
        compiler_params=pltpu.CompilerParams(vmem_limit_bytes=16 * 1024 * 1024),
        cost_estimate=pl.CostEstimate(
            flops=2 * rows * heads * depth * wide, bytes_accessed=4_000_000, transcendentals=0
        ),
        name="values",
    )(*blocks, up)


def write_rows(part, outs, cols):
    at = 0
    for out in outs:
        size = out.shape[0]
        out[:, cols] = part[at : at + size].astype(out.dtype)
        at += size


def project_kernel(*refs, parts):
    count = len(parts)
    given, w_ref, outs, values = refs[:count], refs[count], refs[count + 1 : -1], refs[-1]
    at = 0
    for ref, (first, size) in zip(given, parts):
        values[at : at + size, :] = ref[first : first + size, :]
        at += size
    tile = 512

    @pl.loop(0, w_ref.shape[1] // tile)
    def _(j):
        cols = pl.ds(pl.multiple_of(j * tile, tile), tile)
        write_rows(
            jnp.dot(values[...], w_ref[:, cols], preferred_element_type=jnp.float32), outs, cols
        )


def project(values, out, shapes):
    parts = [(first, size) for _, first, size in values]
    rows = sum(size for _, size in parts)
    depth, width = out.shape
    return pl.pallas_call(
        functools.partial(project_kernel, parts=parts),
        in_specs=[VMEM_SPEC] * (len(values) + 1),
        out_specs=[VMEM_SPEC] * len(shapes),
        out_shape=[jax.ShapeDtypeStruct((r, width), d) for r, d in shapes],
        scratch_shapes=[pltpu.VMEM((rows, depth), jnp.bfloat16)],
        compiler_params=pltpu.CompilerParams(vmem_limit_bytes=16 * 1024 * 1024),
        cost_estimate=pl.CostEstimate(
            flops=2 * rows * depth * width, bytes_accessed=17_000_000, transcendentals=0
        ),
        name="project",
    )(*[v for v, _, _ in values], out)


def feed_kernel(*refs, blocks):
    given, mixes, down_ref = refs[:blocks], refs[blocks : blocks + 2], refs[blocks + 2]
    *outs, rows, hidden = refs[blocks + 3 :]
    at = 0
    for b in given:
        rows[at : at + b.shape[0], :] = b[...]
        at += b.shape[0]
    tiles = mixes[0].shape[0]
    for side, mix in enumerate(mixes):

        @pl.loop(0, tiles)
        def _(j):
            both = jnp.dot(rows[...], mix[j], preferred_element_type=jnp.float32)
            gate, up_part = both[:, :128], both[:, 128:]
            value = gate / (1.0 + jnp.exp(-gate)) * up_part
            at = pl.multiple_of((side * tiles + j) * 128, 128)
            hidden[:, pl.ds(at, 128)] = value.astype(jnp.bfloat16)

    tile = 512

    @pl.loop(0, down_ref.shape[1] // tile)
    def _(j):
        cols = pl.ds(pl.multiple_of(j * tile, tile), tile)
        write_rows(
            jnp.dot(hidden[...], down_ref[:, cols], preferred_element_type=jnp.float32), outs, cols
        )


def feed(blocks, held, shapes):
    rows = sum(b.shape[0] for b in blocks)
    units, width = held[2].shape
    return pl.pallas_call(
        functools.partial(feed_kernel, blocks=len(blocks)),
        in_specs=[VMEM_SPEC] * (len(blocks) + 3),
        out_specs=[VMEM_SPEC] * len(shapes),
        out_shape=[jax.ShapeDtypeStruct((r, width), d) for r, d in shapes],
        scratch_shapes=[
            pltpu.VMEM((rows, width), jnp.bfloat16),
            pltpu.VMEM((rows, units), jnp.bfloat16),
        ],
        compiler_params=pltpu.CompilerParams(vmem_limit_bytes=16 * 1024 * 1024),
        cost_estimate=pl.CostEstimate(
            flops=6 * rows * width * units, bytes_accessed=28_000_000, transcendentals=rows * units
        ),
        name="feed",
    )(*blocks, *held)


def after(value, *others):
    return lax.optimization_barrier((value,) + others)[0]


SMALL = pltpu.CompilerParams(vmem_limit_bytes=16 * 1024 * 1024)


def glue(kernel, name, args, shapes):
    return pl.pallas_call(
        kernel,
        in_specs=[VMEM_SPEC] * len(args),
        out_specs=[VMEM_SPEC] * len(shapes),
        out_shape=[jax.ShapeDtypeStruct(s, d) for s, d in shapes],
        compiler_params=SMALL,
        cost_estimate=pl.CostEstimate(flops=10_000, bytes_accessed=2_000_000, transcendentals=0),
        name=name,
    )(*args)


def flatten_kernel(hidden_ref, out_ref):
    steps = hidden_ref.shape[1]
    for r in range(hidden_ref.shape[0]):
        out_ref[r * steps : (r + 1) * steps, :] = hidden_ref[r].astype(jnp.float32)


def column_loop(width, body):
    tile = 512

    @pl.loop(0, width // tile)
    def _(j):
        body(pl.ds(pl.multiple_of(j * tile, tile), tile))


def fold_kernel(near_ref, back_ref, out_ref):
    def body(cols):
        total = near_ref[:, cols] + back_ref[:, cols].astype(jnp.float32)
        out_ref[:, cols] = total.astype(jnp.bfloat16)

    column_loop(near_ref.shape[1], body)


def fold(near, back):
    (out,) = glue(fold_kernel, "fold", (near, back), [(near.shape, jnp.bfloat16)])
    return out


def norm_kernel(hidden_ref, gain_ref, own_ref, *refs):
    *received, residual_ref, normed_ref, squares = refs
    width = own_ref.shape[1]
    squares[...] = jnp.zeros_like(squares)

    def add(cols):
        total = hidden_ref[:, cols] + own_ref[:, cols]
        for ref in received:
            total = total + ref[:, cols].astype(jnp.float32)
        residual_ref[:, cols] = total
        square = total * total
        for at in range(0, square.shape[1], 128):
            squares[...] += square[:, at : at + 128]

    column_loop(width, add)
    mean = jnp.sum(squares[...], axis=1, keepdims=True) / width
    scale = lax.rsqrt(mean + norm_eps)

    def write(cols):
        normed_ref[:, cols] = (residual_ref[:, cols] * scale * gain_ref[:, cols]).astype(jnp.bfloat16)

    column_loop(width, write)


def norm(own, received, hidden, gain):
    n, width = own.shape
    return pl.pallas_call(
        norm_kernel,
        in_specs=[VMEM_SPEC] * (3 + len(received)),
        out_specs=[VMEM_SPEC] * 2,
        out_shape=[
            jax.ShapeDtypeStruct((n, width), jnp.float32),
            jax.ShapeDtypeStruct((n, width), jnp.bfloat16),
        ],
        scratch_shapes=[pltpu.VMEM((n, 128), jnp.float32)],
        compiler_params=SMALL,
        cost_estimate=pl.CostEstimate(flops=10_000, bytes_accessed=2_000_000, transcendentals=0),
        name="norm",
    )(hidden, gain, own, *received)


def finish_kernel(residual_ref, own_ref, *refs):
    *received, out_ref = refs

    def body(cols):
        total = residual_ref[:, cols] + own_ref[:, cols]
        for ref in received:
            total = total + ref[:, cols].astype(jnp.float32)
        out_ref[:, cols] = total.astype(jnp.bfloat16)

    column_loop(own_ref.shape[1], body)


def page_kernel(partner_ref, request_ref, count_ref, cache_ref, block_ref, offset_ref):
    dp = lax.axis_index("dp")
    offset_ref[0] = jnp.bitwise_xor(partner_ref[dp], dp)
    for k in range(MIG_MAX):
        rows = cache_ref[0, k * PAGE : (k + 1) * PAGE, :]
        block_ref[k] = jnp.where(k < count_ref[0], rows, jnp.zeros_like(rows))


def page_block(partner, moved_request, moved_pages, cache):
    width = cache.shape[2]
    return pl.pallas_call(
        page_kernel,
        grid_spec=pltpu.PrefetchScalarGridSpec(
            num_scalar_prefetch=3,
            grid=(1,),
            in_specs=[pl.BlockSpec((1,) + cache.shape[1:], lambda i, p, r, c: (r[0], 0, 0))],
            out_specs=[
                pl.BlockSpec((MIG_MAX, PAGE, width), lambda i, p, r, c: (0, 0, 0)),
                pl.BlockSpec(memory_space=pltpu.SMEM),
            ],
        ),
        out_shape=[
            jax.ShapeDtypeStruct((MIG_MAX, PAGE, width), cache.dtype),
            jax.ShapeDtypeStruct((1,), jnp.int32),
        ],
        compiler_params=SMALL,
        cost_estimate=pl.CostEstimate(flops=1_000, bytes_accessed=400_000, transcendentals=0),
        name="pages",
    )(partner.reshape(-1), moved_request, moved_pages, in_hbm(cache))


def pick_kernel(offset_ref, mine_ref, other_ref, out_ref, *, bit):
    trade = lax.rem(offset_ref[0] // (1 << bit), 2) == 1

    @pl.when(trade)
    def _():
        out_ref[...] = other_ref[...]

    @pl.when(jnp.logical_not(trade))
    def _():
        out_ref[...] = mine_ref[...]


def page_trade(block, bit):
    return lax.ppermute(block, "dp", [(d, d ^ (1 << bit)) for d in range(8)])


def page_pick(block, other, offset, bit):
    return pl.pallas_call(
        functools.partial(pick_kernel, bit=bit),
        in_specs=[pl.BlockSpec(memory_space=pltpu.SMEM), VMEM_SPEC, VMEM_SPEC],
        out_specs=VMEM_SPEC,
        out_shape=jax.ShapeDtypeStruct(block.shape, block.dtype),
        compiler_params=SMALL,
        cost_estimate=pl.CostEstimate(flops=1_000, bytes_accessed=400_000, transcendentals=0),
        name="pick",
    )(offset, block, other)


def local(
    request_latent_cache,
    lengths,
    queries,
    incoming_keys,
    hidden_in,
    value_up_weight,
    w_out,
    norm_gain,
    w_gate,
    w_up,
    w_down,
    partner,
    moved_request,
    moved_pages,
):
    req_here, steps_here, width = hidden_in.shape
    n = req_here * steps_here
    up_other, out_other, gate_other = swap_cores(value_up_weight), swap_cores(w_out), swap_cores(w_gate)
    turned = jnp.swapaxes(queries, 2, 3)
    own0, own1, own2, own3, go0, go1, go2, go3 = attend(
        lengths, turned, request_latent_cache, incoming_keys, 0, req_here
    )
    near_shapes = [(n, jnp.float32), (n, jnp.float32), (n, jnp.bfloat16), (n, jnp.float32)]
    far_shapes = [(n, jnp.bfloat16)] * N_X

    go1, go3, own2 = after(go1, up_other), after(go3, up_other), after(own2, up_other)
    far_in1, far_in3 = shift(go1, dz=1), shift(go3, dz=-1)
    near2 = shift(own2, dx=2)
    up2, out2 = hold_projection(value_up_weight, up_other, w_out, out_other)
    block, offset = page_block(
        partner, after(moved_request, out2), moved_pages, request_latent_cache
    )
    traded = page_trade(block, 0)
    first = (near2, far_in1, far_in3, out2, gate_other, traded)
    far1 = shift(after(far_in1, *first), dx=1)
    far3 = shift(after(far_in3, *first), dx=3)
    far_in2, far_in0 = shift(after(go2, *first), dz=-1), shift(after(go0, *first), dz=1)
    far2 = shift(far_in2, dx=2)
    near1 = shift(after(own1, far_in0, far_in2), dx=1)
    near3 = shift(after(own3, far_in0, far_in2), dx=3)
    block = page_pick(block, after(traded, *first), offset, 0)
    block = page_pick(block, after(page_trade(block, 1), far_in0, far_in2), offset, 1)
    second = (far_in0, far_in2, far1, far3, block)
    fup_other = swap_cores(after(w_up, *second))
    down_other = swap_cores(after(w_down, *second))
    (hidden32,) = glue(
        flatten_kernel, "flatten", (after(hidden_in, *first),), [((n, width), jnp.float32)]
    )
    gain = norm_gain.reshape(1, width)
    values_a = values_of([after(own0, far_in0), near2], up2)
    values_b = values_of([far_in0, far1], up2)
    values_c = values_of([far2, far3], up2)
    block = page_pick(block, page_trade(after(block, values_a), 2), offset, 2)
    values_b = after(values_b, values_a, fup_other, down_other)
    far = project([(values_b, 0, 2 * n), (values_c, 0, 2 * n)], out2, far_shapes)
    back1, back3 = shift(far[1], dz=-1), shift(far[3], dz=1)
    aside = shift(far[2], dx=-2)
    values_d = values_of([after(near1, far[0], block), near3], up2)
    near = project(
        [(values_a, 0, n), (values_d, 0, n), (values_a, n, n), (values_d, n, n)], out2, near_shapes
    )
    home2 = shift(near[2], dx=-2)
    back2 = shift(aside, dz=1)
    fold1, fold3 = fold(near[1], back1), fold(near[3], back3)
    home1, home3 = shift(fold1, dx=-1), shift(fold3, dx=-3)
    back0 = shift(after(far[0], fold1, fold3), dz=-1)
    held = hold_feed(after(w_gate, fold1, fold3), gate_other, w_up, fup_other, w_down, down_other)
    residual, normed = norm(
        near[0], [back0, back2, after(home1, held[0]), home2, home3], hidden32, gain
    )

    row1, row3 = shift(normed, dx=1), shift(normed, dx=3)
    over, under = shift(normed, dz=1), shift(normed, dz=-1)
    row2 = shift(normed, dx=2)
    far_row1, far_row3 = shift(row1, dz=1), shift(row3, dz=-1)
    far_row2 = shift(after(under, row3), dx=2)
    near = feed([normed, row1, row2, row3], held, near_shapes)
    home2 = shift(near[2], dx=-2)
    far = feed([after(over, near[0]), far_row1, far_row2, far_row3], held, far_shapes)
    back1, back3 = shift(far[1], dz=-1), shift(far[3], dz=1)
    aside, back0 = shift(far[2], dx=-2), shift(far[0], dz=-1)
    fold1, fold3 = fold(near[1], back1), fold(near[3], back3)
    home1, home3 = shift(fold1, dx=-1), shift(fold3, dx=-3)
    back2 = shift(aside, dz=1)
    (out,) = glue(
        finish_kernel, "finish", (residual, near[0], back0, back2, home1, home2, home3),
        [((n, width), jnp.bfloat16)],
    )
    return out.reshape(req_here, steps_here, width), block


def solution(mesh):
    in_specs = (
        P(("dp", "tp"), None, None),
        P(("dp", "tp")),
        P(("dp", "tp"), None, None, None),
        P(("dp", "tp"), None, None),
        P(("dp", "tp"), None, None),
        P("tp", None, None),
        P("tp", None),
        P(),
        P(None, "tp"),
        P(None, "tp"),
        P("tp", None),
        P(None, "tp"),
        P(("dp", "tp")),
        P(("dp", "tp")),
    )
    out_specs = (P(("dp", "tp"), None, None), P(("dp", "tp"), None, None))
    return jax.shard_map(local, mesh=mesh, in_specs=in_specs, out_specs=out_specs, check_vma=False)
```
